32 devices in a mesh: src: 4 (over x, core), rcv: 8 (over z, y).
Axes of the slice: x: 2, y: 2, z: 4, core: 2. Of those that a mesh axis runs over, the one named last changes fastest.
Arguments:
- traces: bfloat16 [1024, 16, 2000], P('rcv', 'src')
- src_index: int32 [256], P('src'), may hold values from 0 to 1023, as said below
- quality: int32 [1024, 16], P('rcv'), may hold values 0 or 1
Outputs:
- xcorr: float32 [256, 201, 1024], P('src', None, 'rcv')
The draws below stay inside these ranges and needn't reach their ends.
Inputs may be any that keep to these rules, and one draw needn't show every extreme that they name: `src_index`: the source numbered j within each group of 64 sources lies in receiver block j mod 8, among channels (j mod 8) * 128 up to that plus 128 - 1.
All inputs are finite; a program needn't handle non-finite values. No bound on the sum of `quality` on one device may be relied on, other than what follows from the above.
Results may differ from the reference program's by a relative error of at most 0.0067.
Values may be sent and summed in bfloat16 or wider, within the bound.
A program may use at most 576 MiB of HBM per device.

```python
import math
import jax
import jax.numpy as jnp
from jax import lax

L = 2000
LAGH = 100
SEG = 16
SRC_DEV = 64
NSRC = 256
RCV_DEV = 128
BLOCKS = 8
CH = 1024


def draw_traces(key, part):
    key_base, key_scale = jax.random.split(key)
    shape = (CH, SEG, L)
    base = jax.random.normal(key_base, shape, jnp.float32)
    scale = jnp.exp(jax.random.uniform(key_scale, (CH, SEG, 1), jnp.float32, 0.0, math.log(10.0)))
    return (base * scale).astype(jnp.bfloat16)


def draw_src_index(key, part):
    number = jnp.arange(NSRC, dtype=jnp.int32)
    within = number % SRC_DEV
    block = within % BLOCKS
    position = jax.random.randint(key, (NSRC,), 0, RCV_DEV, dtype=jnp.int32)
    position = jnp.where(number == 0, 0, position)
    position = jnp.where(number == NSRC - 1, RCV_DEV - 1, position)
    return (block * RCV_DEV + position).astype(jnp.int32)


def touch_ends(result, rng, smallest, high):
    longest = result.shape.index(max(result.shape))
    spots = []
    for shift in (0, 1):
        where = [jax.random.randint(jax.random.fold_in(rng, axis), (), 0, length) for axis, length in enumerate(result.shape)]
        where[longest] = (where[longest] + shift) % result.shape[longest]
        spots.append(tuple(where))
    return result.at[spots[0]].set(smallest).at[spots[1]].set(high)


def setup_inputs(seed: int = 0) -> dict:
    arg_keys = jax.random.split(jax.random.key(seed), 4)
    return {
        "traces": draw_traces(jax.random.fold_in(arg_keys[3], 71), 0),
        "src_index": draw_src_index(jax.random.fold_in(arg_keys[3], 71), 0),
        "quality": touch_ends((jax.random.randint(arg_keys[2], (CH, SEG), 0, 4) < 3).astype(jnp.int32), jax.random.fold_in(arg_keys[2], 1), 0, 1),
    }


def make_tables():
    half = L // 2
    bins = jnp.arange(1, half + 1, dtype=jnp.int32)
    times = jnp.arange(L, dtype=jnp.int32)
    phase = (times[:, None] * bins[None, :] % L).astype(jnp.float32) * (2.0 * math.pi / L)
    forward = jnp.concatenate([jnp.cos(phase), -jnp.sin(phase)], axis=1).astype(jnp.bfloat16)
    lagvals = jnp.arange(-LAGH, LAGH + 1, dtype=jnp.int32)
    phase_lag = (bins[:, None] * lagvals[None, :] % L).astype(jnp.float32) * (2.0 * math.pi / L)
    weights = jnp.where(bins == half, 1.0, 2.0).astype(jnp.float32)[:, None] / jnp.sqrt(jnp.float32(half))
    inverse = jnp.concatenate([weights * jnp.cos(phase_lag), -weights * jnp.sin(phase_lag)], axis=0).astype(jnp.bfloat16)
    return (forward, inverse)

def whiten(samples, forward):
    half = L // 2
    flat = samples.reshape(-1, L)
    spec = jnp.dot(flat, forward, preferred_element_type=jnp.float32)
    real_part = spec[:, :half]
    imag_part = spec[:, half:]
    power = real_part * real_part + imag_part * imag_part
    level = 0.5 * jnp.sqrt(lax.optimization_barrier(jnp.mean(power, axis=1, keepdims=True)) + 1e-06)
    denom = jnp.maximum(jnp.sqrt(power), level)
    white = jnp.concatenate([real_part / denom, imag_part / denom], axis=1).astype(jnp.bfloat16)
    return white.reshape(samples.shape[0], samples.shape[1], L)

def reference(traces, src_index, quality):
    half = L // 2
    forward, inverse = make_tables()
    white = whiten(traces, forward)
    qf = quality.astype(jnp.float32)
    srcw = white[src_index]
    msrc = qf[src_index]
    count = jnp.dot(msrc, qf.T, preferred_element_type=jnp.float32)
    recv = white.astype(jnp.float32) * qf[:, :, None]
    recv_re = recv[:, :, :half]
    recv_im = recv[:, :, half:]
    inv32 = inverse.astype(jnp.float32)
    nblk = srcw.shape[0] // 4
    blocks_w = srcw.reshape(nblk, 4, srcw.shape[1], L)
    blocks_m = msrc.reshape(nblk, 4, msrc.shape[1])

    def one_block(pair):
        sw, ms = pair
        left = sw.astype(jnp.float32) * ms[:, :, None]
        left_re = left[:, :, :half]
        left_im = left[:, :, half:]
        pre = jnp.einsum('isk,jsk->ijk', left_re, recv_re) + jnp.einsum('isk,jsk->ijk', left_im, recv_im)
        pim = jnp.einsum('isk,jsk->ijk', left_im, recv_re) - jnp.einsum('isk,jsk->ijk', left_re, recv_im)
        cross = jnp.concatenate([pre, pim], axis=2).astype(jnp.bfloat16)
        return jnp.einsum('ijk,kt->itj', cross.astype(jnp.float32), inv32)
    lagged = lax.map(one_block, (blocks_w, blocks_m))
    lagged = lagged.reshape(srcw.shape[0], 2 * LAGH + 1, traces.shape[0])
    return lagged / jnp.maximum(count, 1.0)[:, None, :]
```

```python
import functools
import math

import jax
import jax.numpy as jnp
import ml_dtypes
import numpy as np
from jax import lax
from jax.experimental import pallas as pl
from jax.experimental.pallas import tpu as pltpu
from jax.sharding import PartitionSpec as P

LAGH = 100
BINS = 8
GROUPS_STEP = 16
VMEM = 60 * 1024 * 1024


def padded_groups(length):
    groups = -(-(length // 2) // BINS)
    return -(-groups // GROUPS_STEP) * GROUPS_STEP


def make_tables(length):
    half = length // 2
    pad = padded_groups(length) * BINS
    bins = np.arange(1, half + 1)
    unit = np.float32(2.0 * math.pi / length)
    phase = (bins[:, None] * np.arange(length)[None, :] % length).astype(np.float32) * unit
    forward = np.zeros((2, pad, length), np.float32)
    forward[0, :half] = np.cos(phase)
    forward[1, :half] = -np.sin(phase)
    lags = np.arange(-LAGH, LAGH + 1)
    phase = (lags[:, None] * bins[None, :] % length).astype(np.float32) * unit
    weights = np.where(bins == half, 1.0, 2.0).astype(np.float32) / np.sqrt(np.float32(half))
    nlag = 2 * LAGH + 1
    inverse = np.zeros((-(-nlag // 16) * 16, 2, pad), np.float32)
    inverse[:nlag, 0, :half] = weights * np.cos(phase)
    inverse[:nlag, 1, :half] = -weights * np.sin(phase)
    step = GROUPS_STEP * BINS
    inverse = inverse.reshape(-1, 2, pad // step, step).transpose(0, 2, 1, 3)
    inverse = inverse.reshape(-1, 2 * pad)
    return forward.astype(ml_dtypes.bfloat16), inverse.astype(ml_dtypes.bfloat16)


def whiten_kernel(half, seg, forward_ref, traces_ref, quality_ref, out_ref, spec, power):
    step = pl.program_id(0)
    rows = forward_ref.shape[1]
    cols = traces_ref.shape[0]
    width = cols // seg
    part = lax.dot_general(
        forward_ref[...].reshape(2 * rows, -1),
        traces_ref[...],
        (((1,), (1,)), ((), ())),
        preferred_element_type=jnp.float32,
    )
    re, im = part[:rows], part[rows:]
    start = pl.multiple_of(step * rows, rows)
    spec[0, pl.ds(start, rows), :] = re
    spec[1, pl.ds(start, rows), :] = im
    total = jnp.sum((re * re + im * im).reshape(rows // 8, 8, cols), axis=0)

    @pl.when(step == 0)
    def _():
        power[...] = total

    @pl.when(step > 0)
    def _():
        power[...] += total

    @pl.when(step == pl.num_programs(0) - 1)
    def _():
        mean = jnp.sum(power[...], axis=0, keepdims=True) * (1.0 / half)
        level = 0.5 * jnp.sqrt(mean + 1e-06)
        qual = quality_ref[...]

        def one_group(g, carry):
            at = pl.ds(pl.multiple_of(g * BINS, BINS), BINS)
            re, im = spec[0, at, :], spec[1, at, :]
            scale = qual / jnp.maximum(jnp.sqrt(re * re + im * im), level)
            parts = []
            for value in (re * scale, im * scale):
                for s in range(seg):
                    parts.append(value[:, s * width : (s + 1) * width])
            out_ref[g] = jnp.concatenate(parts, axis=0).astype(jnp.bfloat16)
            return carry

        lax.fori_loop(0, out_ref.shape[0], one_group, 0, unroll=4)


def whiten(traces, quality_local, forward):
    rows, seg, length = traces.shape
    pad = forward.shape[1]
    steps = 4
    cols = rows * seg
    return pl.pallas_call(
        functools.partial(whiten_kernel, length // 2, seg),
        grid=(steps,),
        in_specs=[
            pl.BlockSpec((2, pad // steps, length), lambda i: (0, i, 0)),
            pl.BlockSpec((cols, length), lambda i: (0, 0)),
            pl.BlockSpec((1, cols), lambda i: (0, 0)),
        ],
        out_specs=pl.BlockSpec((pad // BINS, 2 * seg * BINS, rows), lambda i: (0, 0, 0)),
        out_shape=jax.ShapeDtypeStruct((pad // BINS, 2 * seg * BINS, rows), jnp.bfloat16),
        scratch_shapes=[
            pltpu.VMEM((2, pad, cols), jnp.float32),
            pltpu.VMEM((8, cols), jnp.float32),
        ],
        compiler_params=pltpu.CompilerParams(vmem_limit_bytes=VMEM),
        name="whiten",
    )(forward, traces.transpose(1, 0, 2).reshape(cols, length), quality_local)


def pick_kernel(onehot_ref, white_ref, out_ref):
    depth = white_ref.shape[0] * white_ref.shape[2]
    for g in range(white_ref.shape[1]):
        block = white_ref[:, g].reshape(depth, -1)
        out_ref[:, g * depth : (g + 1) * depth] = lax.dot_general(
            onehot_ref[...], block, (((1,), (1,)), ((), ())), preferred_element_type=jnp.float32
        )


def pick(onehot, white):
    parts, groups, depth, rows = white.shape
    step = GROUPS_STEP
    return pl.pallas_call(
        pick_kernel,
        grid=(groups // step,),
        in_specs=[
            pl.BlockSpec(onehot.shape, lambda i: (0, 0)),
            pl.BlockSpec((parts, step, depth, rows), lambda i: (0, i, 0, 0)),
        ],
        out_specs=pl.BlockSpec((onehot.shape[0], step * parts * depth), lambda i: (0, i)),
        out_shape=jax.ShapeDtypeStruct((onehot.shape[0], groups * parts * depth), jnp.float32),
        compiler_params=pltpu.CompilerParams(vmem_limit_bytes=VMEM),
        name="pick",
    )(onehot, white)


def correlate_kernel(blocks, white_ref, src_ref, flags_ref, qual_ref, inverse_ref, out_ref, cross):
    step = pl.program_id(0)
    parts, groups, depth, width = white_ref.shape
    full = parts * depth
    nsrc = src_ref.shape[0]
    each = nsrc // blocks
    nlag = out_ref.shape[1]
    half_k = groups * BINS
    lane = lax.broadcasted_iota(jnp.int32, (1, BINS, full), 2)
    row = lax.broadcasted_iota(jnp.int32, (1, BINS, full), 1)
    mask = lane % BINS == row

    def two_groups(t, carry):
        products = []
        for gg in range(2):
            g = 2 * t + gg
            y = white_ref[:, g].reshape(parts, 2, depth // 2, width)
            turned = jnp.concatenate([-y[:, 1:], y[:, :1]], axis=1)
            right = jnp.concatenate([y.reshape(full, width), turned.reshape(full, width)], axis=1)
            x = src_ref[:, pl.ds(pl.multiple_of(g * full, full), full)].astype(jnp.float32)
            left = jnp.where(mask, x[:, None, :], 0.0)
            left = left.reshape(nsrc * BINS, full).astype(jnp.bfloat16)
            prod = jnp.dot(left, right, preferred_element_type=jnp.float32)
            products.append(prod.reshape(nsrc, BINS, 2 * width))
        both = jnp.concatenate(products, axis=1).astype(jnp.bfloat16)
        at = pl.multiple_of(t * 2 * BINS, 2 * BINS)
        cross[:, pl.ds(at, 2 * BINS), :] = both[:, :, :width]
        cross[:, pl.ds(half_k + at, 2 * BINS), :] = both[:, :, width:]
        return carry

    lax.fori_loop(0, groups // 2, two_groups, 0)

    table = inverse_ref[...]

    def place(m):
        return (m % each) * blocks + m // each

    def add_pair(p, first):
        right = jnp.concatenate([cross[2 * p], cross[2 * p + 1]], axis=1)
        lagged = jnp.dot(table, right, preferred_element_type=jnp.float32)
        for h in range(2):
            value = lagged[:nlag, h * width : (h + 1) * width]
            i = place(2 * p + h)
            out_ref[i] = value if first else out_ref[i] + value

    @pl.when(step == 0)
    def _():
        lax.fori_loop(0, nsrc // 2, lambda p, c: (add_pair(p, True), c)[1], 0)

    @pl.when(step > 0)
    def _():
        lax.fori_loop(0, nsrc // 2, lambda p, c: (add_pair(p, False), c)[1], 0)

    @pl.when(step == pl.num_programs(0) - 1)
    def _():
        count = jnp.dot(flags_ref[...], qual_ref[...], preferred_element_type=jnp.float32)
        inv = 1.0 / jnp.maximum(count, 1.0)
        for m in range(nsrc):
            i = place(m)
            out_ref[i] = out_ref[i] * inv[m : m + 1, :]


def correlate(white, src, qual, inverse, blocks):
    parts, groups, depth, rows = white.shape
    nsrc = src.shape[0]
    step = GROUPS_STEP
    nlag = 2 * LAGH + 1
    taps = inverse.shape[0]
    flops = 2 * nsrc * rows * groups * (BINS * parts * depth * 2 + 2 * BINS * taps)
    return pl.pallas_call(
        functools.partial(correlate_kernel, blocks),
        grid=(groups // step,),
        in_specs=[
            pl.BlockSpec((parts, step, depth, rows), lambda i: (0, i, 0, 0)),
            pl.BlockSpec((nsrc, step * parts * depth), lambda i: (0, i)),
            pl.BlockSpec((nsrc, qual.shape[0]), lambda i: (0, groups * parts * depth // 128)),
            pl.BlockSpec(qual.shape, lambda i: (0, 0)),
            pl.BlockSpec((taps, 2 * step * BINS), lambda i: (0, i)),
        ],
        out_specs=pl.BlockSpec((nsrc, nlag, rows), lambda i: (0, 0, 0)),
        out_shape=jax.ShapeDtypeStruct((nsrc, nlag, rows), jnp.float32),
        scratch_shapes=[pltpu.VMEM((nsrc, 2 * step * BINS, rows), jnp.bfloat16)],
        compiler_params=pltpu.CompilerParams(vmem_limit_bytes=VMEM),
        cost_estimate=pl.CostEstimate(flops=flops, bytes_accessed=40_000_000, transcendentals=0),
        name="correlate",
    )(white, src, src, qual, inverse)


def on_device(blocks, traces, src_index, quality):
    rows, seg_local, length = traces.shape
    nsrc = src_index.shape[0]
    each = nsrc // blocks
    forward, inverse = make_tables(length)
    here, part = lax.axis_index("rcv"), lax.axis_index("src")
    mine = lax.dynamic_slice_in_dim(quality, part * seg_local, seg_local, axis=1)
    mine = mine.astype(jnp.float32).T.reshape(1, rows * seg_local)
    white_local = whiten(traces, mine, jnp.asarray(forward))
    white_all = lax.all_gather(white_local, "src", axis=0)
    own = lax.dynamic_index_in_dim(src_index.reshape(each, blocks), here, 1, keepdims=False)
    onehot = (own[:, None] == here * rows + jnp.arange(rows, dtype=jnp.int32)[None, :]).astype(
        jnp.bfloat16
    )
    qual = jnp.pad(quality.astype(jnp.bfloat16), ((0, 0), (0, 128 - quality.shape[1])))
    found = pick(onehot, white_all)
    flags = jnp.dot(onehot, qual, preferred_element_type=jnp.float32)
    sent = jnp.concatenate([found, flags], axis=1).astype(jnp.bfloat16)
    got = lax.all_gather(sent, "rcv", axis=0, tiled=True)
    return correlate(white_all, got, qual.T, jnp.asarray(inverse), blocks)


def solution(mesh):
    return jax.shard_map(
        functools.partial(on_device, mesh.shape["rcv"]),
        mesh=mesh,
        in_specs=(P("rcv", "src", None), P("src"), P("rcv", None)),
        out_specs=P("src", None, "rcv"),
        check_vma=False,
    )
```

```python
import functools
import math

import jax
import jax.numpy as jnp
import ml_dtypes
import numpy as np
from jax import lax
from jax.experimental import pallas as pl
from jax.experimental.pallas import tpu as pltpu
from jax.sharding import PartitionSpec as P

LAGH = 100
BINS = 8
GROUPS_STEP = 16
VMEM = 60 * 1024 * 1024


def padded_groups(length):
    groups = -(-(length // 2 + 1) // BINS)
    return -(-groups // GROUPS_STEP) * GROUPS_STEP


def make_tables(length):
    half = length // 2
    pad = padded_groups(length) * BINS
    bins = np.arange(1, half + 1)
    unit = np.float32(2.0 * math.pi / length)
    phase = (bins[:, None] * np.arange(length)[None, :] % length).astype(np.float32) * unit
    forward = np.zeros((2, pad, length), np.float32)
    forward[0, :half] = np.cos(phase)
    forward[1, :half] = -np.sin(phase)
    lags = np.arange(-LAGH, LAGH + 1)
    phase = (lags[:, None] * bins[None, :] % length).astype(np.float32) * unit
    weights = np.where(bins == half, 1.0, 2.0).astype(np.float32) / np.sqrt(np.float32(half))
    nlag = 2 * LAGH + 1
    inverse = np.zeros((-(-nlag // 16) * 16, 2, pad), np.float32)
    inverse[:nlag, 0, :half] = weights * np.cos(phase)
    inverse[:nlag, 1, :half] = -weights * np.sin(phase)
    step = GROUPS_STEP * BINS
    inverse[nlag, 0, half] = 1.0
    inverse = inverse.reshape(-1, 2, pad // step, step).transpose(2, 0, 1, 3)
    inverse = inverse.reshape(pad // step, -1, 2 * step)
    return forward.astype(ml_dtypes.bfloat16), inverse.astype(ml_dtypes.bfloat16)


def whiten_kernel(half, seg, forward_ref, traces_ref, quality_ref, out_ref, spec, power):
    step = pl.program_id(0)
    rows = forward_ref.shape[1]
    cols = traces_ref.shape[0]
    width = cols // seg
    part = lax.dot_general(
        forward_ref[...].reshape(2 * rows, -1),
        traces_ref[...],
        (((1,), (1,)), ((), ())),
        preferred_element_type=jnp.float32,
    )
    re, im = part[:rows], part[rows:]
    start = pl.multiple_of(step * rows, rows)
    spec[0, pl.ds(start, rows), :] = re
    spec[1, pl.ds(start, rows), :] = im
    total = jnp.sum((re * re + im * im).reshape(rows // 8, 8, cols), axis=0)

    @pl.when(step == 0)
    def _():
        power[...] = total

    @pl.when(step > 0)
    def _():
        power[...] += total

    @pl.when(step == pl.num_programs(0) - 1)
    def _():
        mean = jnp.sum(power[...], axis=0, keepdims=True) * (1.0 / half)
        level = 0.5 * jnp.sqrt(mean + 1e-06)
        qual = quality_ref[...]

        def one_group(g, carry):
            at = pl.ds(pl.multiple_of(g * BINS, BINS), BINS)
            re, im = spec[0, at, :], spec[1, at, :]
            scale = qual / jnp.maximum(jnp.sqrt(re * re + im * im), level)
            parts = []
            for value in (re * scale, im * scale):
                for s in range(seg):
                    parts.append(value[:, s * width : (s + 1) * width])
            out_ref[g] = jnp.concatenate(parts, axis=0).astype(jnp.bfloat16)
            return carry

        lax.fori_loop(0, half // BINS, one_group, 0, unroll=5)
        first = lax.broadcasted_iota(jnp.int32, (BINS, width), 0) == 0
        parts = [jnp.where(first, qual[:, s * width : (s + 1) * width], 0.0) for s in range(seg)]
        parts += [jnp.zeros_like(part) for part in parts]
        out_ref[half // BINS] = jnp.concatenate(parts, axis=0).astype(jnp.bfloat16)
        for g in range(half // BINS + 1, out_ref.shape[0]):
            out_ref[g] = jnp.zeros(out_ref.shape[1:], jnp.bfloat16)


def whiten(traces, quality_local, forward):
    rows, seg, length = traces.shape
    pad = forward.shape[1]
    steps = 4
    cols = rows * seg
    return pl.pallas_call(
        functools.partial(whiten_kernel, length // 2, seg),
        grid=(steps,),
        in_specs=[
            pl.BlockSpec((2, pad // steps, length), lambda i: (0, i, 0)),
            pl.BlockSpec((cols, length), lambda i: (0, 0)),
            pl.BlockSpec((1, cols), lambda i: (0, 0)),
        ],
        out_specs=pl.BlockSpec((pad // BINS, 2 * seg * BINS, rows), lambda i: (0, 0, 0)),
        out_shape=jax.ShapeDtypeStruct((pad // BINS, 2 * seg * BINS, rows), jnp.bfloat16),
        scratch_shapes=[
            pltpu.VMEM((2, pad, cols), jnp.float32),
            pltpu.VMEM((8, cols), jnp.float32),
        ],
        compiler_params=pltpu.CompilerParams(vmem_limit_bytes=VMEM),
        name="whiten",
    )(forward, traces.transpose(1, 0, 2).reshape(cols, length), quality_local)


def other(a, bit):
    low, high = a % 2, a // 2
    return high * 2 + 1 - low if bit == 0 else (1 - high) * 2 + low


def stack_kernel(
    blocks, white_ref, onehot_ref, inverse_ref, out_ref,
    ybuf, xbuf, cross, acc, own_sem, y_send, y_recv, z_send, z_recv, p_send, p_recv,
):
    parts, _, depth, width = ybuf.shape
    full = parts * depth
    _, chunks, rows16, lanes = xbuf.shape
    groups = GROUPS_STEP
    rep = groups * full // lanes
    each = rows16 // rep
    nsrc = each * blocks
    outer = blocks // 2
    nlag = out_ref.shape[0] // nsrc
    half_k = groups * BINS
    a, b = lax.axis_index("src"), lax.axis_index("rcv")
    core, far = other(a, 0), other(a, 1)
    diag = other(far, 0)
    line, side = b // 2, b % 2
    mate = line * 2 + 1 - side

    barrier = pltpu.get_barrier_semaphore()
    peers = [{"src": core}, {"src": far}, {"rcv": mate}]
    peers += [{"rcv": ((line + d) % outer) * 2 + side} for d in range(1, outer)]
    for peer in peers:
        pl.semaphore_signal(barrier, inc=1, device_id=peer, device_id_type=pl.DeviceIdType.MESH)
    pl.semaphore_wait(barrier, len(peers))

    def groups_of(c):
        return pl.ds(c * groups, groups)

    def own_copy():
        return pltpu.make_async_copy(white_ref, ybuf.at[a], own_sem)

    def send(src, dst, send_sem, recv_sem, device):
        return pltpu.make_async_remote_copy(
            src_ref=src, dst_ref=dst, send_sem=send_sem, recv_sem=recv_sem,
            device_id=device, device_id_type=pl.DeviceIdType.MESH,
        )

    def y_copy(c, kind):
        at = groups_of(c)
        if kind == 2:
            src, dst = ybuf.at[far, at], ybuf.at[far, at]
        else:
            src, dst = white_ref.at[at], ybuf.at[a, at]
        return send(
            src, dst, y_send.at[c, kind], y_recv.at[c, kind], {"src": far if kind == 0 else core}
        )

    def y_wait(c, kind):
        at = groups_of(c)
        got = (far, core, diag)[kind]
        send(
            ybuf.at[got, at], ybuf.at[got, at], y_send.at[c, kind], y_recv.at[c, kind],
            {"src": far if kind == 0 else core},
        ).wait_recv()

    def z_copy(c, d):
        there = ((line + d) % outer) * 2 + side
        return send(xbuf.at[b, c], xbuf.at[b, c], z_send.at[c, d], z_recv.at[c, d], {"rcv": there})

    def z_wait(c, d):
        start = ((line + outer - d) % outer) * 2 + side
        send(
            xbuf.at[start, c], xbuf.at[start, c], z_send.at[c, d], z_recv.at[c, d], {"rcv": start}
        ).wait_recv()

    def p_copy(c, d):
        start = ((line + outer - d) % outer) * 2 + side
        return send(
            xbuf.at[start, c], xbuf.at[start, c], p_send.at[c, d], p_recv.at[c, d], {"rcv": mate}
        )

    def p_wait(c, d):
        start = ((line + outer - d) % outer) * 2 + 1 - side
        send(
            xbuf.at[start, c], xbuf.at[start, c], p_send.at[c, d], p_recv.at[c, d], {"rcv": mate}
        ).wait_recv()

    def start_own(c, carry):
        y_copy(c, 0).start()
        y_copy(c, 1).start()
        return carry

    lax.fori_loop(0, chunks, start_own, 0)
    own_copy().start()
    acc[...] = jnp.zeros_like(acc)
    own_copy().wait()

    row16 = lax.broadcasted_iota(jnp.int32, (rows16, full), 0)
    lane = lax.broadcasted_iota(jnp.int32, (1, BINS, full), 2)
    row = lax.broadcasted_iota(jnp.int32, (1, BINS, full), 1)
    mask = lane % BINS == row

    def pick(c):
        for t in range(groups // rep):
            found = None
            for sub in range(rep):
                block = ybuf[:, c * groups + t * rep + sub].reshape(full, width)
                part = lax.dot_general(
                    onehot_ref[...], block, (((1,), (1,)), ((), ())),
                    preferred_element_type=jnp.float32,
                )
                found = part if sub == 0 else jnp.where(row16 // each == sub, part, found)
            xbuf[b, c, :, t * full : (t + 1) * full] = found.astype(jnp.bfloat16)

    def multiply(c):
        def one_step(t, carry):
            x_all = xbuf[:, c, :, pl.ds(pl.multiple_of(t * full, full), full)].astype(jnp.float32)
            for s0 in range(0, rep, 2):
                products = []
                for sub in (s0, s0 + 1):
                    y = ybuf[:, c * groups + t * rep + sub].reshape(parts, 2, depth // 2, width)
                    turned = jnp.concatenate([-y[:, 1:], y[:, :1]], axis=1)
                    right = jnp.concatenate(
                        [y.reshape(full, width), turned.reshape(full, width)], axis=1
                    )
                    left = []
                    for n in range(each):
                        r = sub * each + n
                        left.append(jnp.where(mask, x_all[:, r : r + 1, :], 0.0))
                    left = jnp.concatenate(left, axis=0).reshape(nsrc * BINS, full)
                    prod = jnp.dot(
                        left.astype(jnp.bfloat16), right, preferred_element_type=jnp.float32
                    )
                    products.append(prod.reshape(nsrc, BINS, 2 * width))
                both = jnp.concatenate(products, axis=1).astype(jnp.bfloat16)
                at = pl.multiple_of((t * rep + s0) * BINS, 2 * BINS)
                cross[:, pl.ds(at, 2 * BINS), :] = both[:, :, :width]
                cross[:, pl.ds(half_k + at, 2 * BINS), :] = both[:, :, width:]
            return carry

        lax.fori_loop(0, groups // rep, one_step, 0, unroll=2)

    def invert(c):
        table = inverse_ref[c]

        def add_pair(p, carry):
            right = jnp.concatenate([cross[2 * p], cross[2 * p + 1]], axis=1)
            lagged = jnp.dot(table, right, preferred_element_type=jnp.float32)
            acc[2 * p] += lagged[:, :width]
            acc[2 * p + 1] += lagged[:, width:]
            return carry

        lax.fori_loop(0, nsrc // 2, add_pair, 0, unroll=4)

    def one_chunk(c, carry):
        @pl.when(c < chunks)
        def _():
            y_wait(c, 0)
            y_copy(c, 2).start()

        @pl.when(jnp.logical_and(c >= 1, c <= chunks))
        def _():
            y_wait(c - 1, 1)
            y_wait(c - 1, 2)
            pick(c - 1)
            for d in range(1, outer):
                z_copy(c - 1, d).start()
            p_copy(c - 1, 0).start()

        @pl.when(jnp.logical_and(c >= 2, c <= chunks + 1))
        def _():
            for d in range(1, outer):
                z_wait(c - 2, d)
                p_copy(c - 2, d).start()

        @pl.when(c >= 3)
        def _():
            for d in range(outer):
                p_wait(c - 3, d)
            multiply(c - 3)
            invert(c - 3)

        return carry

    lax.fori_loop(0, chunks + 3, one_chunk, 0)

    def finish(i, carry):
        value = acc[i]
        scale = 1.0 / jnp.maximum(value[nlag : nlag + 1], 1.0)
        out_ref[pl.ds(i, nlag, stride=nsrc), :] = value[:nlag] * scale
        return carry

    lax.fori_loop(0, nsrc, finish, 0)

    def drain(c, carry):
        for kind in range(3):
            y_copy(c, kind).wait_send()
        for d in range(1, outer):
            z_copy(c, d).wait_send()
        for d in range(outer):
            p_copy(c, d).wait_send()
        return carry

    lax.fori_loop(0, chunks, drain, 0)


def stack(white, onehot, inverse, parts, blocks):
    total, depth, rows = white.shape
    chunks, taps, depth_k = inverse.shape
    nlag = 2 * LAGH + 1
    nsrc = blocks * onehot.shape[0]
    rep = 16 // onehot.shape[0]
    lanes = GROUPS_STEP * parts * depth // rep
    outer = blocks // 2
    flops = 2 * nsrc * rows * total * (BINS * parts * depth * 2 + 2 * BINS * taps)
    return pl.pallas_call(
        functools.partial(stack_kernel, blocks),
        in_specs=[
            pl.BlockSpec(memory_space=pl.ANY),
            pl.BlockSpec(memory_space=pltpu.VMEM),
            pl.BlockSpec(memory_space=pltpu.VMEM),
        ],
        out_specs=pl.BlockSpec(memory_space=pltpu.VMEM),
        out_shape=jax.ShapeDtypeStruct((nlag * nsrc, rows), jnp.float32),
        scratch_shapes=[
            pltpu.VMEM((parts, total, depth, rows), jnp.bfloat16),
            pltpu.VMEM((blocks, chunks, 16, lanes), jnp.bfloat16),
            pltpu.VMEM((nsrc, depth_k, rows), jnp.bfloat16),
            pltpu.VMEM((nsrc, taps, rows), jnp.float32),
            pltpu.SemaphoreType.DMA,
            pltpu.SemaphoreType.DMA((chunks, 3)),
            pltpu.SemaphoreType.DMA((chunks, 3)),
            pltpu.SemaphoreType.DMA((chunks, outer)),
            pltpu.SemaphoreType.DMA((chunks, outer)),
            pltpu.SemaphoreType.DMA((chunks, outer)),
            pltpu.SemaphoreType.DMA((chunks, outer)),
        ],
        compiler_params=pltpu.CompilerParams(
            vmem_limit_bytes=VMEM, collective_id=0, has_side_effects=True
        ),
        cost_estimate=pl.CostEstimate(flops=flops, bytes_accessed=20_000_000, transcendentals=0),
        name="stack",
    )(white, jnp.tile(onehot, (rep, 1)), inverse)


def on_device(parts, blocks, traces, src_index, quality):
    rows, seg_local, length = traces.shape
    nsrc = src_index.shape[0]
    each = nsrc // blocks
    forward, inverse = make_tables(length)
    here, part = lax.axis_index("rcv"), lax.axis_index("src")
    mine = lax.dynamic_slice_in_dim(quality, part * seg_local, seg_local, axis=1)
    mine = mine.astype(jnp.float32).T.reshape(1, rows * seg_local)
    white = whiten(traces, mine, jnp.asarray(forward))
    own = lax.dynamic_index_in_dim(src_index.reshape(each, blocks), here, 1, keepdims=False)
    onehot = (own[:, None] == here * rows + jnp.arange(rows, dtype=jnp.int32)[None, :]).astype(
        jnp.bfloat16
    )
    out = stack(white, onehot, jnp.asarray(inverse), parts, blocks)
    return out.reshape(2 * LAGH + 1, nsrc, rows).transpose(1, 0, 2)


def solution(mesh):
    return jax.shard_map(
        functools.partial(on_device, mesh.shape["src"], mesh.shape["rcv"]),
        mesh=mesh,
        in_specs=(P("rcv", "src", None), P("src"), P("rcv", None)),
        out_specs=P("src", None, "rcv"),
        check_vma=False,
    )
```

```python
import functools
import math

import jax
import jax.numpy as jnp
import ml_dtypes
import numpy as np
from jax import lax
from jax.experimental import pallas as pl
from jax.experimental.pallas import tpu as pltpu
from jax.sharding import PartitionSpec as P

LAGH = 100
BINS = 8
GROUPS_STEP = 16
INVERT = 2
VMEM = 60 * 1024 * 1024


def padded_groups(length):
    groups = -(-(length // 2 + 1) // BINS)
    return -(-groups // (GROUPS_STEP * INVERT)) * GROUPS_STEP * INVERT


def make_tables(length):
    half = length // 2
    pad = padded_groups(length) * BINS
    bins = np.arange(1, half + 1)
    unit = np.float32(2.0 * math.pi / length)
    phase = (bins[:, None] * np.arange(length)[None, :] % length).astype(np.float32) * unit
    forward = np.zeros((2, pad, length), np.float32)
    forward[0, :half] = np.cos(phase)
    forward[1, :half] = -np.sin(phase)
    lags = np.arange(-LAGH, LAGH + 1)
    phase = (lags[:, None] * bins[None, :] % length).astype(np.float32) * unit
    weights = np.where(bins == half, 1.0, 2.0).astype(np.float32) / np.sqrt(np.float32(half))
    nlag = 2 * LAGH + 1
    inverse = np.zeros((-(-nlag // 16) * 16, 2, pad), np.float32)
    inverse[:nlag, 0, :half] = weights * np.cos(phase)
    inverse[:nlag, 1, :half] = -weights * np.sin(phase)
    step = GROUPS_STEP * BINS
    inverse[nlag, 0, half] = 1.0
    inverse = inverse.reshape(-1, 2, pad // step // INVERT, INVERT, step).transpose(2, 0, 3, 1, 4)
    inverse = inverse.reshape(pad // step // INVERT, -1, INVERT * 2 * step)
    return forward.astype(ml_dtypes.bfloat16), inverse.astype(ml_dtypes.bfloat16)


def whiten_kernel(half, seg, forward_ref, traces_ref, quality_ref, out_ref, spec, power):
    step = pl.program_id(0)
    rows = forward_ref.shape[1]
    width = traces_ref.shape[2]
    cols = seg * width
    part = lax.dot_general(
        forward_ref[...].reshape(2 * rows, -1),
        jnp.concatenate([traces_ref[s] for s in range(seg)], axis=1),
        (((1,), (0,)), ((), ())),
        preferred_element_type=jnp.float32,
    )
    re, im = part[:rows], part[rows:]
    start = pl.multiple_of(step * rows, rows)
    spec[0, pl.ds(start, rows), :] = re
    spec[1, pl.ds(start, rows), :] = im
    total = jnp.sum((re * re + im * im).reshape(rows // 8, 8, cols), axis=0)

    @pl.when(step == 0)
    def _():
        power[...] = total

    @pl.when(step > 0)
    def _():
        power[...] += total

    @pl.when(step == pl.num_programs(0) - 1)
    def _():
        mean = jnp.sum(power[...], axis=0, keepdims=True) * (1.0 / half)
        level = 0.5 * jnp.sqrt(mean + 1e-06)
        qual = quality_ref[...]

        def one_group(g, carry):
            at = pl.ds(pl.multiple_of(g * BINS, BINS), BINS)
            re, im = spec[0, at, :], spec[1, at, :]
            scale = qual / jnp.maximum(jnp.sqrt(re * re + im * im), level)
            parts = []
            for value in (re * scale, im * scale):
                for s in range(seg):
                    parts.append(value[:, s * width : (s + 1) * width])
            out_ref[g] = jnp.concatenate(parts, axis=0).astype(jnp.bfloat16)
            return carry

        lax.fori_loop(0, half // BINS, one_group, 0, unroll=5)
        first = lax.broadcasted_iota(jnp.int32, (BINS, width), 0) == 0
        parts = [jnp.where(first, qual[:, s * width : (s + 1) * width], 0.0) for s in range(seg)]
        parts += [jnp.zeros_like(part) for part in parts]
        out_ref[half // BINS] = jnp.concatenate(parts, axis=0).astype(jnp.bfloat16)
        for g in range(half // BINS + 1, out_ref.shape[0]):
            out_ref[g] = jnp.zeros(out_ref.shape[1:], jnp.bfloat16)


def whiten(traces, quality_local, forward):
    rows, seg, length = traces.shape
    pad = forward.shape[1]
    steps = 4
    cols = rows * seg
    return pl.pallas_call(
        functools.partial(whiten_kernel, length // 2, seg),
        grid=(steps,),
        in_specs=[
            pl.BlockSpec((2, pad // steps, length), lambda i: (0, i, 0)),
            pl.BlockSpec((seg, length, rows), lambda i: (0, 0, 0)),
            pl.BlockSpec((1, cols), lambda i: (0, 0)),
        ],
        out_specs=pl.BlockSpec((pad // BINS, 2 * seg * BINS, rows), lambda i: (0, 0, 0)),
        out_shape=jax.ShapeDtypeStruct((pad // BINS, 2 * seg * BINS, rows), jnp.bfloat16),
        scratch_shapes=[
            pltpu.VMEM((2, pad, cols), jnp.float32),
            pltpu.VMEM((8, cols), jnp.float32),
        ],
        compiler_params=pltpu.CompilerParams(vmem_limit_bytes=VMEM),
        name="whiten",
    )(forward, traces.transpose(1, 2, 0), quality_local)


def other(a, bit):
    low, high = a % 2, a // 2
    return high * 2 + 1 - low if bit == 0 else (1 - high) * 2 + low


def stack_kernel(
    blocks, white_ref, onehot_ref, inverse_ref, acc,
    ybuf, xbuf, xf, cross, own_sem, y_send, y_recv, z_send, z_recv, p_send, p_recv,
):
    parts, _, depth, width = ybuf.shape
    full = parts * depth
    _, chunks, rows16, lanes = xbuf.shape
    groups = GROUPS_STEP
    rep = groups * full // lanes
    each = rows16 // rep
    nsrc = each * blocks
    outer = blocks // 2
    half_k = groups * BINS
    a, b = lax.axis_index("src"), lax.axis_index("rcv")
    core, far = other(a, 0), other(a, 1)
    diag = other(far, 0)
    line, side = b // 2, b % 2
    mate = line * 2 + 1 - side

    barrier = pltpu.get_barrier_semaphore()
    peers = [{"src": core}, {"src": far}, {"rcv": mate}]
    peers += [{"rcv": ((line + d) % outer) * 2 + side} for d in range(1, outer)]
    for peer in peers:
        pl.semaphore_signal(barrier, inc=1, device_id=peer, device_id_type=pl.DeviceIdType.MESH)
    pl.semaphore_wait(barrier, len(peers))

    def groups_of(c):
        return pl.ds(c * groups, groups)

    def own_copy():
        return pltpu.make_async_copy(white_ref, ybuf.at[a], own_sem)

    def send(src, dst, send_sem, recv_sem, device):
        return pltpu.make_async_remote_copy(
            src_ref=src, dst_ref=dst, send_sem=send_sem, recv_sem=recv_sem,
            device_id=device, device_id_type=pl.DeviceIdType.MESH,
        )

    def y_copy(c, kind):
        at = groups_of(c)
        if kind == 2:
            src, dst = ybuf.at[far, at], ybuf.at[far, at]
        else:
            src, dst = white_ref.at[at], ybuf.at[a, at]
        return send(
            src, dst, y_send.at[c, kind], y_recv.at[c, kind], {"src": far if kind == 0 else core}
        )

    def y_wait(c, kind):
        at = groups_of(c)
        got = (far, core, diag)[kind]
        send(
            ybuf.at[got, at], ybuf.at[got, at], y_send.at[c, kind], y_recv.at[c, kind],
            {"src": far if kind == 0 else core},
        ).wait_recv()

    def z_copy(c, d):
        there = ((line + d) % outer) * 2 + side
        return send(xbuf.at[b, c], xbuf.at[b, c], z_send.at[c, d], z_recv.at[c, d], {"rcv": there})

    def z_wait(c, d):
        start = ((line + outer - d) % outer) * 2 + side
        send(
            xbuf.at[start, c], xbuf.at[start, c], z_send.at[c, d], z_recv.at[c, d], {"rcv": start}
        ).wait_recv()

    def p_copy(c, d):
        start = ((line + outer - d) % outer) * 2 + side
        return send(
            xbuf.at[start, c], xbuf.at[start, c], p_send.at[c, d], p_recv.at[c, d], {"rcv": mate}
        )

    def p_wait(c, d):
        start = ((line + outer - d) % outer) * 2 + 1 - side
        send(
            xbuf.at[start, c], xbuf.at[start, c], p_send.at[c, d], p_recv.at[c, d], {"rcv": mate}
        ).wait_recv()

    def start_own(c, carry):
        y_copy(c, 0).start()
        y_copy(c, 1).start()
        return carry

    lax.fori_loop(0, chunks, start_own, 0)
    own_copy().start()
    acc[...] = jnp.zeros_like(acc)
    own_copy().wait()

    row16 = lax.broadcasted_iota(jnp.int32, (rows16, full), 0)
    lane = lax.broadcasted_iota(jnp.int32, (BINS, full), 1)
    row = lax.broadcasted_iota(jnp.int32, (BINS, full), 0)
    mask = lane % BINS == row

    def pick(c):
        for t in range(groups // rep):
            found = None
            for sub in range(rep):
                block = ybuf[:, c * groups + t * rep + sub].reshape(full, width)
                part = lax.dot_general(
                    onehot_ref[...], block, (((1,), (1,)), ((), ())),
                    preferred_element_type=jnp.float32,
                )
                found = part if sub == 0 else jnp.where(row16 // each == sub, part, found)
            xbuf[b, c, :, t * full : (t + 1) * full] = found.astype(jnp.bfloat16)

    def multiply(c):
        xf[...] = xbuf[:, c].astype(jnp.float32)

        def one_step(t, carry):
            cols = pl.ds(pl.multiple_of(t * full, full), full)
            for s0 in range(0, rep, 2):
                products = []
                for sub in (s0, s0 + 1):
                    y = ybuf[:, c * groups + t * rep + sub].reshape(parts, 2, depth // 2, width)
                    turned = jnp.concatenate([-y[:, 1:], y[:, :1]], axis=1)
                    right = jnp.concatenate(
                        [y.reshape(full, width), turned.reshape(full, width)], axis=1
                    )
                    left = []
                    for n in range(each):
                        r = sub * each + n
                        for k in range(blocks):
                            left.append(jnp.where(mask, xf[k, r : r + 1, cols], 0.0))
                    left = jnp.concatenate(left, axis=0)
                    prod = jnp.dot(
                        left.astype(jnp.bfloat16), right, preferred_element_type=jnp.float32
                    )
                    products.append(prod.reshape(nsrc, BINS, 2 * width))
                both = jnp.concatenate(products, axis=1).astype(jnp.bfloat16)
                at = pl.multiple_of(c % INVERT * 2 * half_k + (t * rep + s0) * BINS, 2 * BINS)
                cross[:, pl.ds(at, 2 * BINS), :] = both[:, :, :width]
                cross[:, pl.ds(half_k + at, 2 * BINS), :] = both[:, :, width:]
            return carry

        lax.fori_loop(0, groups // rep, one_step, 0, unroll=2)

    def invert(c):
        table = inverse_ref[c // INVERT]

        def add_pair(p, carry):
            right = jnp.concatenate([cross[2 * p], cross[2 * p + 1]], axis=1)
            lagged = jnp.dot(table, right, preferred_element_type=jnp.float32)
            acc[2 * p] += lagged[:, :width]
            acc[2 * p + 1] += lagged[:, width:]
            return carry

        lax.fori_loop(0, nsrc // 2, add_pair, 0, unroll=4)

    def one_chunk(c, carry):
        @pl.when(c < chunks)
        def _():
            y_wait(c, 0)
            y_copy(c, 2).start()

        @pl.when(jnp.logical_and(c >= 1, c <= chunks))
        def _():
            y_wait(c - 1, 1)
            y_wait(c - 1, 2)
            pick(c - 1)
            for d in range(1, outer):
                z_copy(c - 1, d).start()
            p_copy(c - 1, 0).start()

        @pl.when(jnp.logical_and(c >= 2, c <= chunks + 1))
        def _():
            for d in range(1, outer):
                z_wait(c - 2, d)
                p_copy(c - 2, d).start()

        @pl.when(c >= 3)
        def _():
            for d in range(outer):
                p_wait(c - 3, d)
            multiply(c - 3)

            @pl.when((c - 3) % INVERT == INVERT - 1)
            def _():
                invert(c - 3)

        return carry

    lax.fori_loop(0, chunks + 3, one_chunk, 0)

    def drain(c, carry):
        for kind in range(3):
            y_copy(c, kind).wait_send()
        for d in range(1, outer):
            z_copy(c, d).wait_send()
        for d in range(outer):
            p_copy(c, d).wait_send()
        return carry

    lax.fori_loop(0, chunks, drain, 0)


def stack(white, onehot, inverse, parts, blocks):
    total, depth, rows = white.shape
    steps, taps, depth_k = inverse.shape
    chunks = steps * INVERT
    nsrc = blocks * onehot.shape[0]
    rep = 16 // onehot.shape[0]
    lanes = GROUPS_STEP * parts * depth // rep
    outer = blocks // 2
    flops = 2 * nsrc * rows * total * (BINS * parts * depth * 2 + 2 * BINS * taps)
    return pl.pallas_call(
        functools.partial(stack_kernel, blocks),
        in_specs=[
            pl.BlockSpec(memory_space=pl.ANY),
            pl.BlockSpec(memory_space=pltpu.VMEM),
            pl.BlockSpec(memory_space=pltpu.VMEM),
        ],
        out_specs=pl.BlockSpec(memory_space=pltpu.VMEM),
        out_shape=jax.ShapeDtypeStruct((nsrc, taps, rows), jnp.float32),
        scratch_shapes=[
            pltpu.VMEM((parts, total, depth, rows), jnp.bfloat16),
            pltpu.VMEM((blocks, chunks, 16, lanes), jnp.bfloat16),
            pltpu.VMEM((blocks, 16, lanes), jnp.float32),
            pltpu.VMEM((nsrc, depth_k, rows), jnp.bfloat16),
            pltpu.SemaphoreType.DMA,
            pltpu.SemaphoreType.DMA((chunks, 3)),
            pltpu.SemaphoreType.DMA((chunks, 3)),
            pltpu.SemaphoreType.DMA((chunks, outer)),
            pltpu.SemaphoreType.DMA((chunks, outer)),
            pltpu.SemaphoreType.DMA((chunks, outer)),
            pltpu.SemaphoreType.DMA((chunks, outer)),
        ],
        compiler_params=pltpu.CompilerParams(
            vmem_limit_bytes=VMEM, collective_id=0, has_side_effects=True
        ),
        cost_estimate=pl.CostEstimate(flops=flops, bytes_accessed=20_000_000, transcendentals=0),
        name="stack",
    )(white, jnp.tile(onehot, (rep, 1)), inverse)


def finish_kernel(acc_ref, out_ref):
    nlag = out_ref.shape[0]
    for n in range(acc_ref.shape[0]):
        count = acc_ref[n, nlag : nlag + 1, :]
        out_ref[:, n, :] = acc_ref[n, :nlag, :] * (1.0 / jnp.maximum(count, 1.0))


def finish(acc):
    nsrc, taps, rows = acc.shape
    nlag, tile = 2 * LAGH + 1, 8
    return pl.pallas_call(
        finish_kernel,
        grid=(nsrc // tile,),
        in_specs=[pl.BlockSpec((tile, taps, rows), lambda i: (i, 0, 0))],
        out_specs=pl.BlockSpec((nlag, tile, rows), lambda i: (0, i, 0)),
        out_shape=jax.ShapeDtypeStruct((nlag, nsrc, rows), jnp.float32),
        name="finish",
    )(acc)


def on_device(parts, blocks, traces, src_index, quality):
    rows, seg_local, length = traces.shape
    nsrc = src_index.shape[0]
    each = nsrc // blocks
    forward, inverse = make_tables(length)
    here, part = lax.axis_index("rcv"), lax.axis_index("src")
    mine = lax.dynamic_slice_in_dim(quality.T, part * seg_local, seg_local, axis=0)
    mine = mine.astype(jnp.float32).reshape(1, rows * seg_local)
    white = whiten(traces, mine, jnp.asarray(forward))
    own = lax.dynamic_index_in_dim(src_index.reshape(each, blocks), here, 1, keepdims=False)
    onehot = (own[:, None] == here * rows + jnp.arange(rows, dtype=jnp.int32)[None, :]).astype(
        jnp.bfloat16
    )
    return finish(stack(white, onehot, jnp.asarray(inverse), parts, blocks)).transpose(1, 0, 2)


def solution(mesh):
    return jax.shard_map(
        functools.partial(on_device, mesh.shape["src"], mesh.shape["rcv"]),
        mesh=mesh,
        in_specs=(P("rcv", "src", None), P("src"), P("rcv", None)),
        out_specs=P("src", None, "rcv"),
        check_vma=False,
    )
```

```python
import functools
import math

import jax
import jax.numpy as jnp
import ml_dtypes
import numpy as np
from jax import lax
from jax.experimental import pallas as pl
from jax.experimental.pallas import tpu as pltpu
from jax.sharding import PartitionSpec as P

LAGH = 100
BINS = 8
GROUPS_STEP = 8
INVERT = 4
AHEAD = 4
VMEM = 60 * 1024 * 1024


def padded_groups(length):
    groups = -(-(length // 2 + 1) // BINS)
    return -(-groups // (GROUPS_STEP * INVERT)) * GROUPS_STEP * INVERT


def make_tables(length):
    half = length // 2
    pad = padded_groups(length) * BINS
    bins = np.arange(1, half + 1)
    unit = np.float32(2.0 * math.pi / length)
    phase = (bins[:, None] * np.arange(length)[None, :] % length).astype(np.float32) * unit
    forward = np.zeros((2, pad, length), np.float32)
    forward[0, :half] = np.cos(phase)
    forward[1, :half] = -np.sin(phase)
    lags = np.arange(-LAGH, LAGH + 1)
    phase = (lags[:, None] * bins[None, :] % length).astype(np.float32) * unit
    weights = np.where(bins == half, 1.0, 2.0).astype(np.float32) / np.sqrt(np.float32(half))
    nlag = 2 * LAGH + 1
    inverse = np.zeros((-(-nlag // 16) * 16, 2, pad), np.float32)
    inverse[:nlag, 0, :half] = weights * np.cos(phase)
    inverse[:nlag, 1, :half] = -weights * np.sin(phase)
    step = GROUPS_STEP * BINS
    inverse[nlag, 0, half] = 1.0
    inverse = inverse.reshape(-1, 2, pad // step // INVERT, INVERT, step).transpose(2, 0, 3, 1, 4)
    inverse = inverse.reshape(pad // step // INVERT, -1, INVERT * 2 * step)
    return forward.astype(ml_dtypes.bfloat16), inverse.astype(ml_dtypes.bfloat16)


def whiten_kernel(half, seg, forward_ref, traces_ref, quality_ref, out_ref, spec, power):
    step = pl.program_id(0)
    rows = forward_ref.shape[1]
    width = traces_ref.shape[2]
    cols = seg * width
    part = lax.dot_general(
        forward_ref[...].reshape(2 * rows, -1),
        jnp.concatenate([traces_ref[s] for s in range(seg)], axis=1),
        (((1,), (0,)), ((), ())),
        preferred_element_type=jnp.float32,
    )
    re, im = part[:rows], part[rows:]
    start = pl.multiple_of(step * rows, rows)
    spec[0, pl.ds(start, rows), :] = re
    spec[1, pl.ds(start, rows), :] = im
    total = jnp.sum((re * re + im * im).reshape(rows // 8, 8, cols), axis=0)

    @pl.when(step == 0)
    def _():
        power[...] = total

    @pl.when(step > 0)
    def _():
        power[...] += total

    @pl.when(step == pl.num_programs(0) - 1)
    def _():
        mean = jnp.sum(power[...], axis=0, keepdims=True) * (1.0 / half)
        level = 0.5 * jnp.sqrt(mean + 1e-06)
        first_row = lax.axis_index("src") * seg
        qual = jnp.concatenate(
            [quality_ref[pl.ds(first_row + s, 1), :] for s in range(seg)], axis=1
        ).astype(jnp.float32)

        def one_group(g, carry):
            at = pl.ds(pl.multiple_of(g * BINS, BINS), BINS)
            re, im = spec[0, at, :], spec[1, at, :]
            scale = qual / jnp.maximum(jnp.sqrt(re * re + im * im), level)
            parts = []
            for value in (re * scale, im * scale):
                for s in range(seg):
                    parts.append(value[:, s * width : (s + 1) * width])
            out_ref[g] = jnp.concatenate(parts, axis=0).astype(jnp.bfloat16)
            return carry

        lax.fori_loop(0, half // BINS, one_group, 0, unroll=5)
        first = lax.broadcasted_iota(jnp.int32, (BINS, width), 0) == 0
        parts = [jnp.where(first, qual[:, s * width : (s + 1) * width], 0.0) for s in range(seg)]
        parts += [jnp.zeros_like(part) for part in parts]
        out_ref[half // BINS] = jnp.concatenate(parts, axis=0).astype(jnp.bfloat16)
        for g in range(half // BINS + 1, out_ref.shape[0]):
            out_ref[g] = jnp.zeros(out_ref.shape[1:], jnp.bfloat16)


def whiten(traces, quality, forward):
    rows, seg, length = traces.shape
    pad = forward.shape[1]
    steps = 4
    cols = rows * seg
    return pl.pallas_call(
        functools.partial(whiten_kernel, length // 2, seg),
        grid=(steps,),
        in_specs=[
            pl.BlockSpec((2, pad // steps, length), lambda i: (0, i, 0)),
            pl.BlockSpec((seg, length, rows), lambda i: (0, 0, 0)),
            pl.BlockSpec((quality.shape[1], rows), lambda i: (0, 0)),
        ],
        out_specs=pl.BlockSpec((pad // BINS, 2 * seg * BINS, rows), lambda i: (0, 0, 0)),
        out_shape=jax.ShapeDtypeStruct((pad // BINS, 2 * seg * BINS, rows), jnp.bfloat16),
        scratch_shapes=[
            pltpu.VMEM((2, pad, cols), jnp.float32),
            pltpu.VMEM((8, cols), jnp.float32),
        ],
        compiler_params=pltpu.CompilerParams(vmem_limit_bytes=VMEM),
        name="whiten",
    )(forward, traces.transpose(1, 2, 0), quality.T)


def other(a, bit):
    low, high = a % 2, a // 2
    return high * 2 + 1 - low if bit == 0 else (1 - high) * 2 + low


def stack_kernel(
    blocks, each, white_ref, index_ref, inverse_ref, acc,
    ybuf, xbuf, xf, cross, own_sem, y_send, y_recv, z_send, z_recv, p_send, p_recv,
):
    parts, _, depth, width = ybuf.shape
    full = parts * depth
    _, chunks, rows16, lanes = xbuf.shape
    groups = GROUPS_STEP
    rep = groups * full // lanes
    nsrc = each * blocks
    outer = blocks // 2
    half_k = groups * BINS
    a, b = lax.axis_index("src"), lax.axis_index("rcv")
    core, far = other(a, 0), other(a, 1)
    diag = other(far, 0)
    line, side = b // 2, b % 2
    mate = line * 2 + 1 - side

    barrier = pltpu.get_barrier_semaphore()
    peers = [{"src": core}, {"src": far}, {"rcv": mate}]
    peers += [{"rcv": ((line + d) % outer) * 2 + side} for d in range(1, outer)]
    for peer in peers:
        pl.semaphore_signal(barrier, inc=1, device_id=peer, device_id_type=pl.DeviceIdType.MESH)
    pl.semaphore_wait(barrier, len(peers))

    def groups_of(c):
        return pl.ds(c * groups, groups)

    def own_copy():
        return pltpu.make_async_copy(white_ref, ybuf.at[a], own_sem)

    def send(src, dst, send_sem, recv_sem, device):
        return pltpu.make_async_remote_copy(
            src_ref=src, dst_ref=dst, send_sem=send_sem, recv_sem=recv_sem,
            device_id=device, device_id_type=pl.DeviceIdType.MESH,
        )

    def y_copy(c, kind):
        at = groups_of(c)
        if kind == 2:
            src, dst = ybuf.at[far, at], ybuf.at[far, at]
        else:
            src, dst = white_ref.at[at], ybuf.at[a, at]
        return send(
            src, dst, y_send.at[c, kind], y_recv.at[c, kind], {"src": far if kind == 0 else core}
        )

    def y_wait(c, kind):
        at = groups_of(c)
        got = (far, core, diag)[kind]
        send(
            ybuf.at[got, at], ybuf.at[got, at], y_send.at[c, kind], y_recv.at[c, kind],
            {"src": far if kind == 0 else core},
        ).wait_recv()

    def z_copy(c, d):
        there = ((line + d) % outer) * 2 + side
        return send(xbuf.at[b, c], xbuf.at[b, c], z_send.at[c, d], z_recv.at[c, d], {"rcv": there})

    def z_wait(c, d):
        start = ((line + outer - d) % outer) * 2 + side
        send(
            xbuf.at[start, c], xbuf.at[start, c], z_send.at[c, d], z_recv.at[c, d], {"rcv": start}
        ).wait_recv()

    def p_copy(c, d):
        start = ((line + outer - d) % outer) * 2 + side
        return send(
            xbuf.at[start, c], xbuf.at[start, c], p_send.at[c, d], p_recv.at[c, d], {"rcv": mate}
        )

    def p_wait(c, d):
        start = ((line + outer - d) % outer) * 2 + 1 - side
        send(
            xbuf.at[start, c], xbuf.at[start, c], p_send.at[c, d], p_recv.at[c, d], {"rcv": mate}
        ).wait_recv()

    def start_own(c, carry):
        y_copy(c, 0).start()
        y_copy(c, 1).start()
        return carry

    lax.fori_loop(0, AHEAD, start_own, 0)
    own_copy().start()
    acc[...] = jnp.zeros_like(acc)
    own_copy().wait()

    row16 = lax.broadcasted_iota(jnp.int32, (rows16, full), 0)
    lane = lax.broadcasted_iota(jnp.int32, (BINS, full), 1)
    row = lax.broadcasted_iota(jnp.int32, (BINS, full), 0)
    mask = lane % BINS == row

    source = jnp.zeros((rows16, width), jnp.int32)
    number = lax.broadcasted_iota(jnp.int32, (rows16, width), 0) % each
    for n in range(each):
        source = jnp.where(number == n, index_ref[n * blocks + b], source)
    channel = b * width + lax.broadcasted_iota(jnp.int32, (rows16, width), 1)
    onehot = jnp.where(source == channel, 1.0, 0.0).astype(jnp.bfloat16)

    def pick(c):
        for t in range(groups // rep):
            found = None
            for sub in range(rep):
                block = ybuf[:, c * groups + t * rep + sub].reshape(full, width)
                part = lax.dot_general(
                    onehot, block, (((1,), (1,)), ((), ())),
                    preferred_element_type=jnp.float32,
                )
                found = part if sub == 0 else jnp.where(row16 // each == sub, part, found)
            xbuf[b, c, :, t * full : (t + 1) * full] = found.astype(jnp.bfloat16)

    def multiply(c):
        xf[...] = xbuf[:, c].astype(jnp.float32)

        def one_step(t, carry):
            cols = pl.ds(pl.multiple_of(t * full, full), full)
            for s0 in range(0, rep, 2):
                products = []
                for sub in (s0, s0 + 1):
                    y = ybuf[:, c * groups + t * rep + sub].reshape(parts, 2, depth // 2, width)
                    turned = jnp.concatenate([-y[:, 1:], y[:, :1]], axis=1)
                    right = jnp.concatenate(
                        [y.reshape(full, width), turned.reshape(full, width)], axis=1
                    )
                    left = []
                    for n in range(each):
                        r = sub * each + n
                        for k in range(blocks):
                            left.append(jnp.where(mask, xf[k, r : r + 1, cols], 0.0))
                    left = jnp.concatenate(left, axis=0)
                    prod = jnp.dot(
                        left.astype(jnp.bfloat16), right, preferred_element_type=jnp.float32
                    )
                    products.append(prod.reshape(nsrc, BINS, 2 * width))
                both = jnp.concatenate(products, axis=1).astype(jnp.bfloat16)
                at = pl.multiple_of(c % INVERT * 2 * half_k + (t * rep + s0) * BINS, 2 * BINS)
                cross[:, pl.ds(at, 2 * BINS), :] = both[:, :, :width]
                cross[:, pl.ds(half_k + at, 2 * BINS), :] = both[:, :, width:]
            return carry

        lax.fori_loop(0, groups // rep, one_step, 0, unroll=True)

    def invert(c):
        table = inverse_ref[c // INVERT]

        def add_pair(p, carry):
            right = jnp.concatenate([cross[2 * p], cross[2 * p + 1]], axis=1)
            lagged = jnp.dot(table, right, preferred_element_type=jnp.float32)
            acc[2 * p] += lagged[:, :width]
            acc[2 * p + 1] += lagged[:, width:]
            return carry

        lax.fori_loop(0, nsrc // 2, add_pair, 0, unroll=4)

    def one_chunk(c, carry):
        @pl.when(c < chunks - AHEAD)
        def _():
            start_own(c + AHEAD, 0)

        @pl.when(c < chunks)
        def _():
            y_wait(c, 0)
            y_copy(c, 2).start()

        @pl.when(jnp.logical_and(c >= 1, c <= chunks))
        def _():
            y_wait(c - 1, 1)
            y_wait(c - 1, 2)
            pick(c - 1)
            for d in range(1, outer):
                z_copy(c - 1, d).start()
            p_copy(c - 1, 0).start()

        @pl.when(jnp.logical_and(c >= 2, c <= chunks + 1))
        def _():
            for d in range(1, outer):
                z_wait(c - 2, d)
                p_copy(c - 2, d).start()

        @pl.when(c >= 3)
        def _():
            for d in range(outer):
                p_wait(c - 3, d)
            multiply(c - 3)

            @pl.when((c - 3) % INVERT == INVERT - 1)
            def _():
                invert(c - 3)

        return carry

    lax.fori_loop(0, chunks + 3, one_chunk, 0)

    def drain(c, carry):
        for kind in range(3):
            y_copy(c, kind).wait_send()
        for d in range(1, outer):
            z_copy(c, d).wait_send()
        for d in range(outer):
            p_copy(c, d).wait_send()
        return carry

    lax.fori_loop(0, chunks, drain, 0)


def stack(white, src_index, inverse, parts, blocks):
    total, depth, rows = white.shape
    steps, taps, depth_k = inverse.shape
    chunks = steps * INVERT
    nsrc = src_index.shape[0]
    each = nsrc // blocks
    rep = 16 // each
    lanes = GROUPS_STEP * parts * depth // rep
    outer = blocks // 2
    flops = 2 * nsrc * rows * total * (BINS * parts * depth * 2 + 2 * BINS * taps)
    return pl.pallas_call(
        functools.partial(stack_kernel, blocks, each),
        in_specs=[
            pl.BlockSpec(memory_space=pl.ANY),
            pl.BlockSpec(memory_space=pltpu.SMEM),
            pl.BlockSpec(memory_space=pltpu.VMEM),
        ],
        out_specs=pl.BlockSpec(memory_space=pltpu.VMEM),
        out_shape=jax.ShapeDtypeStruct((nsrc, taps, rows), jnp.float32),
        scratch_shapes=[
            pltpu.VMEM((parts, total, depth, rows), jnp.bfloat16),
            pltpu.VMEM((blocks, chunks, 16, lanes), jnp.bfloat16),
            pltpu.VMEM((blocks, 16, lanes), jnp.float32),
            pltpu.VMEM((nsrc, depth_k, rows), jnp.bfloat16),
            pltpu.SemaphoreType.DMA,
            pltpu.SemaphoreType.DMA((chunks, 3)),
            pltpu.SemaphoreType.DMA((chunks, 3)),
            pltpu.SemaphoreType.DMA((chunks, outer)),
            pltpu.SemaphoreType.DMA((chunks, outer)),
            pltpu.SemaphoreType.DMA((chunks, outer)),
            pltpu.SemaphoreType.DMA((chunks, outer)),
        ],
        compiler_params=pltpu.CompilerParams(
            vmem_limit_bytes=VMEM, collective_id=0, has_side_effects=True
        ),
        cost_estimate=pl.CostEstimate(flops=flops, bytes_accessed=20_000_000, transcendentals=0),
        name="stack",
    )(white, src_index, inverse)


def finish_kernel(acc_ref, out_ref):
    nlag = out_ref.shape[0]
    value = acc_ref[...]
    scale = 1.0 / jnp.maximum(value[:, nlag : nlag + 1, :], 1.0)
    out_ref[...] = jnp.swapaxes(value * scale, 0, 1)[:nlag]


def finish(acc):
    nsrc, taps, rows = acc.shape
    nlag, tile = 2 * LAGH + 1, 8
    return pl.pallas_call(
        finish_kernel,
        grid=(nsrc // tile,),
        in_specs=[pl.BlockSpec((tile, taps, rows), lambda i: (i, 0, 0))],
        out_specs=pl.BlockSpec((nlag, tile, rows), lambda i: (0, i, 0)),
        out_shape=jax.ShapeDtypeStruct((nlag, nsrc, rows), jnp.float32),
        name="finish",
    )(acc)


def on_device(parts, blocks, traces, src_index, quality):
    forward, inverse = make_tables(traces.shape[2])
    white = whiten(traces, quality, jnp.asarray(forward))
    return finish(stack(white, src_index, jnp.asarray(inverse), parts, blocks)).transpose(1, 0, 2)


def solution(mesh):
    return jax.shard_map(
        functools.partial(on_device, mesh.shape["src"], mesh.shape["rcv"]),
        mesh=mesh,
        in_specs=(P("rcv", "src", None), P("src"), P("rcv", None)),
        out_specs=P("src", None, "rcv"),
        check_vma=False,
    )
```

```python
import functools
import math

import jax
import jax.numpy as jnp
import ml_dtypes
import numpy as np
from jax import lax
from jax.experimental import pallas as pl
from jax.experimental.pallas import tpu as pltpu
from jax.sharding import PartitionSpec as P

LAGH = 100
BINS = 8
GROUPS_STEP = 16
INVERT = 2
VMEM = 60 * 1024 * 1024


def padded_groups(length):
    groups = -(-(length // 2 + 1) // BINS)
    return -(-groups // (GROUPS_STEP * INVERT)) * GROUPS_STEP * INVERT


def make_tables(length):
    half = length // 2
    pad = padded_groups(length) * BINS
    bins = np.arange(1, half + 1)
    unit = np.float32(2.0 * math.pi / length)
    phase = (bins[:, None] * np.arange(length)[None, :] % length).astype(np.float32) * unit
    forward = np.zeros((2, pad, length), np.float32)
    forward[0, :half] = np.cos(phase)
    forward[1, :half] = -np.sin(phase)
    lags = np.arange(-LAGH, LAGH + 1)
    phase = (lags[:, None] * bins[None, :] % length).astype(np.float32) * unit
    weights = np.where(bins == half, 1.0, 2.0).astype(np.float32) / np.sqrt(np.float32(half))
    nlag = 2 * LAGH + 1
    inverse = np.zeros((-(-nlag // 16) * 16, 2, pad), np.float32)
    inverse[:nlag, 0, :half] = weights * np.cos(phase)
    inverse[:nlag, 1, :half] = -weights * np.sin(phase)
    step = GROUPS_STEP * BINS
    inverse[nlag, 0, half] = 1.0
    inverse = inverse.reshape(-1, 2, pad // step // INVERT, INVERT, step).transpose(2, 0, 3, 1, 4)
    inverse = inverse.reshape(pad // step // INVERT, -1, INVERT * 2 * step)
    return forward.astype(ml_dtypes.bfloat16), inverse.astype(ml_dtypes.bfloat16)


def whiten_kernel(half, seg, forward_ref, traces_ref, quality_ref, out_ref, spec, power):
    step = pl.program_id(0)
    rows = forward_ref.shape[1]
    width = traces_ref.shape[2]
    cols = seg * width
    part = lax.dot_general(
        forward_ref[...].reshape(2 * rows, -1),
        jnp.concatenate([traces_ref[s] for s in range(seg)], axis=1),
        (((1,), (0,)), ((), ())),
        preferred_element_type=jnp.float32,
    )
    re, im = part[:rows], part[rows:]
    start = pl.multiple_of(step * rows, rows)
    spec[0, pl.ds(start, rows), :] = re
    spec[1, pl.ds(start, rows), :] = im
    total = jnp.sum((re * re + im * im).reshape(rows // 8, 8, cols), axis=0)

    @pl.when(step == 0)
    def _():
        power[...] = total

    @pl.when(step > 0)
    def _():
        power[...] += total

    @pl.when(step == pl.num_programs(0) - 1)
    def _():
        mean = jnp.sum(power[...], axis=0, keepdims=True) * (1.0 / half)
        level = 0.5 * jnp.sqrt(mean + 1e-06)
        first_row = lax.axis_index("src") * seg
        qual = jnp.concatenate(
            [quality_ref[pl.ds(first_row + s, 1), :] for s in range(seg)], axis=1
        ).astype(jnp.float32)

        def one_group(g, carry):
            at = pl.ds(pl.multiple_of(g * BINS, BINS), BINS)
            re, im = spec[0, at, :], spec[1, at, :]
            scale = qual / jnp.maximum(jnp.sqrt(re * re + im * im), level)
            parts = []
            for value in (re * scale, im * scale):
                for s in range(seg):
                    parts.append(value[:, s * width : (s + 1) * width])
            out_ref[g] = jnp.concatenate(parts, axis=0).astype(jnp.bfloat16)
            return carry

        lax.fori_loop(0, half // BINS, one_group, 0, unroll=5)
        first = lax.broadcasted_iota(jnp.int32, (BINS, width), 0) == 0
        parts = [jnp.where(first, qual[:, s * width : (s + 1) * width], 0.0) for s in range(seg)]
        parts += [jnp.zeros_like(part) for part in parts]
        out_ref[half // BINS] = jnp.concatenate(parts, axis=0).astype(jnp.bfloat16)
        for g in range(half // BINS + 1, out_ref.shape[0]):
            out_ref[g] = jnp.zeros(out_ref.shape[1:], jnp.bfloat16)


def whiten(traces, quality, forward):
    rows, seg, length = traces.shape
    pad = forward.shape[1]
    steps = 4
    cols = rows * seg
    return pl.pallas_call(
        functools.partial(whiten_kernel, length // 2, seg),
        grid=(steps,),
        in_specs=[
            pl.BlockSpec((2, pad // steps, length), lambda i: (0, i, 0)),
            pl.BlockSpec((seg, length, rows), lambda i: (0, 0, 0)),
            pl.BlockSpec((quality.shape[1], rows), lambda i: (0, 0)),
        ],
        out_specs=pl.BlockSpec((pad // BINS, 2 * seg * BINS, rows), lambda i: (0, 0, 0)),
        out_shape=jax.ShapeDtypeStruct((pad // BINS, 2 * seg * BINS, rows), jnp.bfloat16),
        scratch_shapes=[
            pltpu.VMEM((2, pad, cols), jnp.float32),
            pltpu.VMEM((8, cols), jnp.float32),
        ],
        compiler_params=pltpu.CompilerParams(vmem_limit_bytes=VMEM),
        name="whiten",
    )(forward, traces.transpose(1, 2, 0), quality.T)


def other(a, bit):
    low, high = a % 2, a // 2
    return high * 2 + 1 - low if bit == 0 else (1 - high) * 2 + low


def stack_kernel(
    blocks, each, white_ref, index_ref, inverse_ref, acc,
    ybuf, xbuf, xf, cross, own_sem, y_send, y_recv, z_send, z_recv, p_send, p_recv,
):
    parts, _, depth, width = ybuf.shape
    full = parts * depth
    _, chunks, rows16, lanes = xbuf.shape
    groups = GROUPS_STEP
    rep = groups * full // lanes
    nsrc = each * blocks
    outer = blocks // 2
    half_k = groups * BINS
    a, b = lax.axis_index("src"), lax.axis_index("rcv")
    core, far = other(a, 0), other(a, 1)
    diag = other(far, 0)
    line, side = b // 2, b % 2
    mate = line * 2 + 1 - side

    barrier = pltpu.get_barrier_semaphore()
    peers = [{"src": core}, {"src": far}, {"rcv": mate}]
    peers += [{"rcv": ((line + d) % outer) * 2 + side} for d in range(1, outer)]
    for peer in peers:
        pl.semaphore_signal(barrier, inc=1, device_id=peer, device_id_type=pl.DeviceIdType.MESH)
    pl.semaphore_wait(barrier, len(peers))

    def groups_of(c):
        return pl.ds(c * groups, groups)

    def own_copy():
        return pltpu.make_async_copy(white_ref, ybuf.at[a], own_sem)

    def send(src, dst, send_sem, recv_sem, device):
        return pltpu.make_async_remote_copy(
            src_ref=src, dst_ref=dst, send_sem=send_sem, recv_sem=recv_sem,
            device_id=device, device_id_type=pl.DeviceIdType.MESH,
        )

    def y_copy(c, kind):
        at = groups_of(c)
        if kind == 2:
            src, dst = ybuf.at[far, at], ybuf.at[far, at]
        else:
            src, dst = white_ref.at[at], ybuf.at[a, at]
        return send(
            src, dst, y_send.at[c, kind], y_recv.at[c, kind], {"src": far if kind == 0 else core}
        )

    def y_wait(c, kind):
        at = groups_of(c)
        got = (far, core, diag)[kind]
        send(
            ybuf.at[got, at], ybuf.at[got, at], y_send.at[c, kind], y_recv.at[c, kind],
            {"src": far if kind == 0 else core},
        ).wait_recv()

    def z_copy(c, d):
        there = ((line + d) % outer) * 2 + side
        return send(xbuf.at[b, c], xbuf.at[b, c], z_send.at[c, d], z_recv.at[c, d], {"rcv": there})

    def z_wait(c, d):
        start = ((line + outer - d) % outer) * 2 + side
        send(
            xbuf.at[start, c], xbuf.at[start, c], z_send.at[c, d], z_recv.at[c, d], {"rcv": start}
        ).wait_recv()

    def p_copy(c, d):
        start = ((line + outer - d) % outer) * 2 + side
        return send(
            xbuf.at[start, c], xbuf.at[start, c], p_send.at[c, d], p_recv.at[c, d], {"rcv": mate}
        )

    def p_wait(c, d):
        start = ((line + outer - d) % outer) * 2 + 1 - side
        send(
            xbuf.at[start, c], xbuf.at[start, c], p_send.at[c, d], p_recv.at[c, d], {"rcv": mate}
        ).wait_recv()

    def start_own(c, carry):
        y_copy(c, 0).start()
        y_copy(c, 1).start()
        return carry

    lax.fori_loop(0, chunks, start_own, 0)
    own_copy().start()
    acc[...] = jnp.zeros_like(acc)
    own_copy().wait()

    row16 = lax.broadcasted_iota(jnp.int32, (rows16, full), 0)
    lane = lax.broadcasted_iota(jnp.int32, (BINS, full), 1)
    row = lax.broadcasted_iota(jnp.int32, (BINS, full), 0)
    mask = lane % BINS == row

    source = jnp.zeros((rows16, width), jnp.int32)
    number = lax.broadcasted_iota(jnp.int32, (rows16, width), 0) % each
    for n in range(each):
        source = jnp.where(number == n, index_ref[n * blocks + b], source)
    channel = b * width + lax.broadcasted_iota(jnp.int32, (rows16, width), 1)
    onehot = jnp.where(source == channel, 1.0, 0.0).astype(jnp.bfloat16)

    def pick(c):
        for t in range(groups // rep):
            found = None
            for sub in range(rep):
                block = ybuf[:, c * groups + t * rep + sub].reshape(full, width)
                part = lax.dot_general(
                    onehot, block, (((1,), (1,)), ((), ())),
                    preferred_element_type=jnp.float32,
                )
                found = part if sub == 0 else jnp.where(row16 // each == sub, part, found)
            xbuf[b, c, :, t * full : (t + 1) * full] = found.astype(jnp.bfloat16)

    def multiply(c):
        xf[...] = xbuf[:, c].astype(jnp.float32)

        def one_step(t, carry):
            cols = pl.ds(pl.multiple_of(t * full, full), full)
            for sub in range(rep):
                y = ybuf[:, c * groups + t * rep + sub].reshape(parts, 2, depth // 2, width)
                turned = jnp.concatenate([-y[:, 1:], y[:, :1]], axis=1)
                right = jnp.concatenate(
                    [y.reshape(full, width), turned.reshape(full, width)], axis=1
                )
                left = []
                for n in range(each):
                    r = sub * each + n
                    for k in range(blocks):
                        left.append(jnp.where(mask, xf[k, r : r + 1, cols], 0.0))
                left = jnp.concatenate(left, axis=0).astype(jnp.bfloat16)
                prod = jnp.dot(left, right, preferred_element_type=jnp.float32)
                prod = prod.reshape(nsrc, BINS, 2 * width)
                at = pl.multiple_of(c % INVERT * 2 * half_k + (t * rep + sub) * BINS, BINS)
                cross[:, pl.ds(at, BINS), :] = prod[:, :, :width]
                cross[:, pl.ds(half_k + at, BINS), :] = prod[:, :, width:]
            return carry

        lax.fori_loop(0, groups // rep, one_step, 0, unroll=2)

    def invert(c):
        table = inverse_ref[c // INVERT]

        def add_pair(p, carry):
            right = jnp.concatenate([cross[2 * p], cross[2 * p + 1]], axis=1).astype(jnp.bfloat16)
            lagged = jnp.dot(table, right, preferred_element_type=jnp.float32)
            acc[2 * p] += lagged[:, :width]
            acc[2 * p + 1] += lagged[:, width:]
            return carry

        lax.fori_loop(0, nsrc // 2, add_pair, 0, unroll=4)

    def one_chunk(c, carry):
        @pl.when(c < chunks)
        def _():
            y_wait(c, 0)
            y_copy(c, 2).start()

        @pl.when(jnp.logical_and(c >= 1, c <= chunks))
        def _():
            y_wait(c - 1, 1)
            y_wait(c - 1, 2)
            pick(c - 1)
            for d in range(1, outer):
                z_copy(c - 1, d).start()
            p_copy(c - 1, 0).start()

        @pl.when(jnp.logical_and(c >= 2, c <= chunks + 1))
        def _():
            for d in range(1, outer):
                z_wait(c - 2, d)
                p_copy(c - 2, d).start()

        @pl.when(c >= 3)
        def _():
            for d in range(outer):
                p_wait(c - 3, d)
            multiply(c - 3)

            @pl.when((c - 3) % INVERT == INVERT - 1)
            def _():
                invert(c - 3)

        return carry

    lax.fori_loop(0, chunks + 3, one_chunk, 0)

    def drain(c, carry):
        for kind in range(3):
            y_copy(c, kind).wait_send()
        for d in range(1, outer):
            z_copy(c, d).wait_send()
        for d in range(outer):
            p_copy(c, d).wait_send()
        return carry

    lax.fori_loop(0, chunks, drain, 0)


def stack(white, src_index, inverse, parts, blocks):
    total, depth, rows = white.shape
    steps, taps, depth_k = inverse.shape
    chunks = steps * INVERT
    nsrc = src_index.shape[0]
    each = nsrc // blocks
    rep = 16 // each
    lanes = GROUPS_STEP * parts * depth // rep
    outer = blocks // 2
    flops = 2 * nsrc * rows * total * (BINS * parts * depth * 2 + 2 * BINS * taps)
    return pl.pallas_call(
        functools.partial(stack_kernel, blocks, each),
        in_specs=[
            pl.BlockSpec(memory_space=pl.ANY),
            pl.BlockSpec(memory_space=pltpu.SMEM),
            pl.BlockSpec(memory_space=pltpu.VMEM),
        ],
        out_specs=pl.BlockSpec(memory_space=pltpu.VMEM),
        out_shape=jax.ShapeDtypeStruct((nsrc, taps, rows), jnp.float32),
        scratch_shapes=[
            pltpu.VMEM((parts, total, depth, rows), jnp.bfloat16),
            pltpu.VMEM((blocks, chunks, 16, lanes), jnp.bfloat16),
            pltpu.VMEM((blocks, 16, lanes), jnp.float32),
            pltpu.VMEM((nsrc, depth_k, rows), jnp.float32),
            pltpu.SemaphoreType.DMA,
            pltpu.SemaphoreType.DMA((chunks, 3)),
            pltpu.SemaphoreType.DMA((chunks, 3)),
            pltpu.SemaphoreType.DMA((chunks, outer)),
            pltpu.SemaphoreType.DMA((chunks, outer)),
            pltpu.SemaphoreType.DMA((chunks, outer)),
            pltpu.SemaphoreType.DMA((chunks, outer)),
        ],
        compiler_params=pltpu.CompilerParams(
            vmem_limit_bytes=VMEM, collective_id=0, has_side_effects=True
        ),
        cost_estimate=pl.CostEstimate(flops=flops, bytes_accessed=20_000_000, transcendentals=0),
        name="stack",
    )(white, src_index, inverse)


def finish_kernel(acc_ref, out_ref):
    nlag = out_ref.shape[0]
    value = acc_ref[...]
    scale = 1.0 / jnp.maximum(value[:, nlag : nlag + 1, :], 1.0)
    out_ref[...] = jnp.swapaxes(value * scale, 0, 1)[:nlag]


def finish(acc):
    nsrc, taps, rows = acc.shape
    nlag, tile = 2 * LAGH + 1, 16
    return pl.pallas_call(
        finish_kernel,
        grid=(nsrc // tile,),
        in_specs=[pl.BlockSpec((tile, taps, rows), lambda i: (i, 0, 0))],
        out_specs=pl.BlockSpec((nlag, tile, rows), lambda i: (0, i, 0)),
        out_shape=jax.ShapeDtypeStruct((nlag, nsrc, rows), jnp.float32),
        compiler_params=pltpu.CompilerParams(vmem_limit_bytes=VMEM),
        name="finish",
    )(acc)


def on_device(parts, blocks, traces, src_index, quality):
    forward, inverse = make_tables(traces.shape[2])
    white = whiten(traces, quality, jnp.asarray(forward))
    return finish(stack(white, src_index, jnp.asarray(inverse), parts, blocks)).transpose(1, 0, 2)


def solution(mesh):
    return jax.shard_map(
        functools.partial(on_device, mesh.shape["src"], mesh.shape["rcv"]),
        mesh=mesh,
        in_specs=(P("rcv", "src", None), P("src"), P("rcv", None)),
        out_specs=P("src", None, "rcv"),
        check_vma=False,
    )
```

```python
import functools
import math

import jax
import jax.numpy as jnp
import ml_dtypes
import numpy as np
from jax import lax
from jax.experimental import pallas as pl
from jax.experimental.pallas import tpu as pltpu
from jax.sharding import PartitionSpec as P

LAGH = 100
BINS = 8
GROUPS_STEP = 8
INVERT = 4
VMEM = 60 * 1024 * 1024


def padded_groups(length):
    groups = -(-(length // 2 + 1) // BINS)
    return -(-groups // (GROUPS_STEP * INVERT)) * GROUPS_STEP * INVERT


def make_tables(length):
    half = length // 2
    pad = padded_groups(length) * BINS
    bins = np.arange(1, half + 1)
    unit = np.float32(2.0 * math.pi / length)
    phase = (bins[:, None] * np.arange(length)[None, :] % length).astype(np.float32) * unit
    forward = np.zeros((2, pad, length), np.float32)
    forward[0, :half] = np.cos(phase)
    forward[1, :half] = -np.sin(phase)
    lags = np.arange(-LAGH, LAGH + 1)
    phase = (lags[:, None] * bins[None, :] % length).astype(np.float32) * unit
    weights = np.where(bins == half, 1.0, 2.0).astype(np.float32) / np.sqrt(np.float32(half))
    nlag = 2 * LAGH + 1
    inverse = np.zeros((-(-nlag // 16) * 16, 2, pad), np.float32)
    inverse[:nlag, 0, :half] = weights * np.cos(phase)
    inverse[:nlag, 1, :half] = -weights * np.sin(phase)
    step = GROUPS_STEP * BINS
    inverse[nlag, 0, half] = 1.0
    inverse = inverse.reshape(-1, 2, pad // step // INVERT, INVERT, step).transpose(2, 0, 3, 1, 4)
    inverse = inverse.reshape(pad // step // INVERT, -1, INVERT * 2 * step)
    return forward.astype(ml_dtypes.bfloat16), inverse.astype(ml_dtypes.bfloat16)


def whiten_kernel(half, seg, forward_ref, traces_ref, quality_ref, out_ref, spec, power):
    step = pl.program_id(0)
    rows = forward_ref.shape[1]
    width = traces_ref.shape[2]
    cols = seg * width
    part = lax.dot_general(
        forward_ref[...].reshape(2 * rows, -1),
        jnp.concatenate([traces_ref[s] for s in range(seg)], axis=1),
        (((1,), (0,)), ((), ())),
        preferred_element_type=jnp.float32,
    )
    re, im = part[:rows], part[rows:]
    start = pl.multiple_of(step * rows, rows)
    spec[0, pl.ds(start, rows), :] = re
    spec[1, pl.ds(start, rows), :] = im
    total = jnp.sum((re * re + im * im).reshape(rows // 8, 8, cols), axis=0)

    @pl.when(step == 0)
    def _():
        power[...] = total

    @pl.when(step > 0)
    def _():
        power[...] += total

    @pl.when(step == pl.num_programs(0) - 1)
    def _():
        mean = jnp.sum(power[...], axis=0, keepdims=True) * (1.0 / half)
        level = 0.5 * jnp.sqrt(mean + 1e-06)
        first_row = lax.axis_index("src") * seg
        qual = jnp.concatenate(
            [quality_ref[pl.ds(first_row + s, 1), :] for s in range(seg)], axis=1
        ).astype(jnp.float32)

        def one_group(g, carry):
            at = pl.ds(pl.multiple_of(g * BINS, BINS), BINS)
            re, im = spec[0, at, :], spec[1, at, :]
            scale = qual / jnp.maximum(jnp.sqrt(re * re + im * im), level)
            parts = []
            for value in (re * scale, im * scale):
                for s in range(seg):
                    parts.append(value[:, s * width : (s + 1) * width])
            out_ref[g] = jnp.concatenate(parts, axis=0).astype(jnp.bfloat16)
            return carry

        lax.fori_loop(0, half // BINS, one_group, 0, unroll=5)
        first = lax.broadcasted_iota(jnp.int32, (BINS, width), 0) == 0
        parts = [jnp.where(first, qual[:, s * width : (s + 1) * width], 0.0) for s in range(seg)]
        parts += [jnp.zeros_like(part) for part in parts]
        out_ref[half // BINS] = jnp.concatenate(parts, axis=0).astype(jnp.bfloat16)
        for g in range(half // BINS + 1, out_ref.shape[0]):
            out_ref[g] = jnp.zeros(out_ref.shape[1:], jnp.bfloat16)


def whiten(traces, quality, forward):
    rows, seg, length = traces.shape
    pad = forward.shape[1]
    steps = 4
    cols = rows * seg
    return pl.pallas_call(
        functools.partial(whiten_kernel, length // 2, seg),
        grid=(steps,),
        in_specs=[
            pl.BlockSpec((2, pad // steps, length), lambda i: (0, i, 0)),
            pl.BlockSpec((seg, length, rows), lambda i: (0, 0, 0)),
            pl.BlockSpec((quality.shape[1], rows), lambda i: (0, 0)),
        ],
        out_specs=pl.BlockSpec((pad // BINS, 2 * seg * BINS, rows), lambda i: (0, 0, 0)),
        out_shape=jax.ShapeDtypeStruct((pad // BINS, 2 * seg * BINS, rows), jnp.bfloat16),
        scratch_shapes=[
            pltpu.VMEM((2, pad, cols), jnp.float32),
            pltpu.VMEM((8, cols), jnp.float32),
        ],
        compiler_params=pltpu.CompilerParams(vmem_limit_bytes=VMEM),
        name="whiten",
    )(forward, traces.transpose(1, 2, 0), quality.T)


def other(a, bit):
    low, high = a % 2, a // 2
    return high * 2 + 1 - low if bit == 0 else (1 - high) * 2 + low


def stack_kernel(
    blocks, each, white_ref, index_ref, inverse_ref, acc,
    ybuf, xbuf, xf, cross, own_sem, y_send, y_recv, z_send, z_recv, p_send, p_recv,
):
    parts, _, depth, width = ybuf.shape
    full = parts * depth
    _, chunks, rows16, lanes = xbuf.shape
    groups = GROUPS_STEP
    rep = groups * full // lanes
    nsrc = each * blocks
    outer = blocks // 2
    half_k = groups * BINS
    a, b = lax.axis_index("src"), lax.axis_index("rcv")
    core, far = other(a, 0), other(a, 1)
    diag = other(far, 0)
    line, side = b // 2, b % 2
    mate = line * 2 + 1 - side

    barrier = pltpu.get_barrier_semaphore()
    peers = [{"src": core}, {"src": far}, {"rcv": mate}]
    peers += [{"rcv": ((line + d) % outer) * 2 + side} for d in range(1, outer)]
    for peer in peers:
        pl.semaphore_signal(barrier, inc=1, device_id=peer, device_id_type=pl.DeviceIdType.MESH)
    pl.semaphore_wait(barrier, len(peers))

    def groups_of(c):
        return pl.ds(c * groups, groups)

    def own_copy():
        return pltpu.make_async_copy(white_ref, ybuf.at[a], own_sem)

    def send(src, dst, send_sem, recv_sem, device):
        return pltpu.make_async_remote_copy(
            src_ref=src, dst_ref=dst, send_sem=send_sem, recv_sem=recv_sem,
            device_id=device, device_id_type=pl.DeviceIdType.MESH,
        )

    def y_copy(c, kind):
        at = groups_of(c)
        if kind == 2:
            src, dst = ybuf.at[far, at], ybuf.at[far, at]
        else:
            src, dst = white_ref.at[at], ybuf.at[a, at]
        return send(
            src, dst, y_send.at[c, kind], y_recv.at[c, kind], {"src": far if kind == 0 else core}
        )

    def y_wait(c, kind):
        at = groups_of(c)
        got = (far, core, diag)[kind]
        send(
            ybuf.at[got, at], ybuf.at[got, at], y_send.at[c, kind], y_recv.at[c, kind],
            {"src": far if kind == 0 else core},
        ).wait_recv()

    def z_copy(c, d):
        there = ((line + d) % outer) * 2 + side
        return send(xbuf.at[b, c], xbuf.at[b, c], z_send.at[c, d], z_recv.at[c, d], {"rcv": there})

    def z_wait(c, d):
        start = ((line + outer - d) % outer) * 2 + side
        send(
            xbuf.at[start, c], xbuf.at[start, c], z_send.at[c, d], z_recv.at[c, d], {"rcv": start}
        ).wait_recv()

    def p_copy(c, d):
        start = ((line + outer - d) % outer) * 2 + side
        return send(
            xbuf.at[start, c], xbuf.at[start, c], p_send.at[c, d], p_recv.at[c, d], {"rcv": mate}
        )

    def p_wait(c, d):
        start = ((line + outer - d) % outer) * 2 + 1 - side
        send(
            xbuf.at[start, c], xbuf.at[start, c], p_send.at[c, d], p_recv.at[c, d], {"rcv": mate}
        ).wait_recv()

    def start_own(c, carry):
        y_copy(c, 0).start()
        y_copy(c, 1).start()
        return carry

    lax.fori_loop(0, chunks, start_own, 0)
    own_copy().start()
    acc[...] = jnp.zeros_like(acc)
    own_copy().wait()

    row16 = lax.broadcasted_iota(jnp.int32, (rows16, full), 0)
    lane = lax.broadcasted_iota(jnp.int32, (BINS, full), 1)
    row = lax.broadcasted_iota(jnp.int32, (BINS, full), 0)
    mask = lane % BINS == row

    source = jnp.zeros((rows16, width), jnp.int32)
    number = lax.broadcasted_iota(jnp.int32, (rows16, width), 0) % each
    for n in range(each):
        source = jnp.where(number == n, index_ref[n * blocks + b], source)
    channel = b * width + lax.broadcasted_iota(jnp.int32, (rows16, width), 1)
    onehot = jnp.where(source == channel, 1.0, 0.0).astype(jnp.bfloat16)

    def pick(c):
        for t in range(groups // rep):
            found = None
            for sub in range(rep):
                block = ybuf[:, c * groups + t * rep + sub].reshape(full, width)
                part = lax.dot_general(
                    onehot, block, (((1,), (1,)), ((), ())),
                    preferred_element_type=jnp.float32,
                )
                found = part if sub == 0 else jnp.where(row16 // each == sub, part, found)
            xbuf[b, c, :, t * full : (t + 1) * full] = found.astype(jnp.bfloat16)

    def multiply(c):
        xf[...] = xbuf[:, c].astype(jnp.float32)

        def one_step(t, carry):
            cols = pl.ds(pl.multiple_of(t * full, full), full)
            for sub in range(rep):
                y = ybuf[:, c * groups + t * rep + sub].reshape(parts, 2, depth // 2, width)
                turned = jnp.concatenate([-y[:, 1:], y[:, :1]], axis=1)
                right = jnp.concatenate(
                    [y.reshape(full, width), turned.reshape(full, width)], axis=1
                )
                left = []
                for n in range(each):
                    r = sub * each + n
                    for k in range(blocks):
                        left.append(jnp.where(mask, xf[k, r : r + 1, cols], 0.0))
                left = jnp.concatenate(left, axis=0).astype(jnp.bfloat16)
                prod = jnp.dot(left, right, preferred_element_type=jnp.float32)
                prod = prod.reshape(nsrc, BINS, 2 * width)
                at = pl.multiple_of(c % INVERT * 2 * half_k + (t * rep + sub) * BINS, BINS)
                cross[:, pl.ds(at, BINS), :] = prod[:, :, :width]
                cross[:, pl.ds(half_k + at, BINS), :] = prod[:, :, width:]
            return carry

        lax.fori_loop(0, groups // rep, one_step, 0, unroll=2)

    def invert(c):
        table = inverse_ref[c // INVERT]

        def add_pair(p, carry):
            right = jnp.concatenate([cross[2 * p], cross[2 * p + 1]], axis=1).astype(jnp.bfloat16)
            lagged = jnp.dot(table, right, preferred_element_type=jnp.float32)
            acc[2 * p] += lagged[:, :width]
            acc[2 * p + 1] += lagged[:, width:]
            return carry

        lax.fori_loop(0, nsrc // 2, add_pair, 0, unroll=4)

    def one_chunk(c, carry):
        @pl.when(c < chunks)
        def _():
            y_wait(c, 0)
            y_copy(c, 2).start()

        @pl.when(jnp.logical_and(c >= 1, c <= chunks))
        def _():
            y_wait(c - 1, 1)
            y_wait(c - 1, 2)
            pick(c - 1)
            for d in range(1, outer):
                z_copy(c - 1, d).start()
            p_copy(c - 1, 0).start()

        @pl.when(jnp.logical_and(c >= 2, c <= chunks + 1))
        def _():
            for d in range(1, outer):
                z_wait(c - 2, d)
                p_copy(c - 2, d).start()

        @pl.when(c >= 3)
        def _():
            for d in range(outer):
                p_wait(c - 3, d)
            multiply(c - 3)

            @pl.when((c - 3) % INVERT == INVERT - 1)
            def _():
                invert(c - 3)

        return carry

    lax.fori_loop(0, chunks + 3, one_chunk, 0)

    def drain(c, carry):
        for kind in range(3):
            y_copy(c, kind).wait_send()
        for d in range(1, outer):
            z_copy(c, d).wait_send()
        for d in range(outer):
            p_copy(c, d).wait_send()
        return carry

    lax.fori_loop(0, chunks, drain, 0)


def stack(white, src_index, inverse, parts, blocks):
    total, depth, rows = white.shape
    steps, taps, depth_k = inverse.shape
    chunks = steps * INVERT
    nsrc = src_index.shape[0]
    each = nsrc // blocks
    rep = 16 // each
    lanes = GROUPS_STEP * parts * depth // rep
    outer = blocks // 2
    flops = 2 * nsrc * rows * total * (BINS * parts * depth * 2 + 2 * BINS * taps)
    return pl.pallas_call(
        functools.partial(stack_kernel, blocks, each),
        in_specs=[
            pl.BlockSpec(memory_space=pl.ANY),
            pl.BlockSpec(memory_space=pltpu.SMEM),
            pl.BlockSpec(memory_space=pltpu.VMEM),
        ],
        out_specs=pl.BlockSpec(memory_space=pltpu.VMEM),
        out_shape=jax.ShapeDtypeStruct((nsrc, taps, rows), jnp.float32),
        scratch_shapes=[
            pltpu.VMEM((parts, total, depth, rows), jnp.bfloat16),
            pltpu.VMEM((blocks, chunks, 16, lanes), jnp.bfloat16),
            pltpu.VMEM((blocks, 16, lanes), jnp.float32),
            pltpu.VMEM((nsrc, depth_k, rows), jnp.float32),
            pltpu.SemaphoreType.DMA,
            pltpu.SemaphoreType.DMA((chunks, 3)),
            pltpu.SemaphoreType.DMA((chunks, 3)),
            pltpu.SemaphoreType.DMA((chunks, outer)),
            pltpu.SemaphoreType.DMA((chunks, outer)),
            pltpu.SemaphoreType.DMA((chunks, outer)),
            pltpu.SemaphoreType.DMA((chunks, outer)),
        ],
        compiler_params=pltpu.CompilerParams(
            vmem_limit_bytes=VMEM, collective_id=0, has_side_effects=True
        ),
        cost_estimate=pl.CostEstimate(flops=flops, bytes_accessed=20_000_000, transcendentals=0),
        name="stack",
    )(white, src_index, inverse)


def finish_kernel(acc_ref, out_ref):
    nlag = out_ref.shape[0]
    value = acc_ref[...]
    scale = 1.0 / jnp.maximum(value[:, nlag : nlag + 1, :], 1.0)
    out_ref[...] = jnp.swapaxes(value * scale, 0, 1)[:nlag]


def finish(acc):
    nsrc, taps, rows = acc.shape
    nlag, tile = 2 * LAGH + 1, 16
    return pl.pallas_call(
        finish_kernel,
        grid=(nsrc // tile,),
        in_specs=[pl.BlockSpec((tile, taps, rows), lambda i: (i, 0, 0))],
        out_specs=pl.BlockSpec((nlag, tile, rows), lambda i: (0, i, 0)),
        out_shape=jax.ShapeDtypeStruct((nlag, nsrc, rows), jnp.float32),
        compiler_params=pltpu.CompilerParams(vmem_limit_bytes=VMEM),
        name="finish",
    )(acc)


def on_device(parts, blocks, traces, src_index, quality):
    forward, inverse = make_tables(traces.shape[2])
    white = whiten(traces, quality, jnp.asarray(forward))
    return finish(stack(white, src_index, jnp.asarray(inverse), parts, blocks)).transpose(1, 0, 2)


def solution(mesh):
    return jax.shard_map(
        functools.partial(on_device, mesh.shape["src"], mesh.shape["rcv"]),
        mesh=mesh,
        in_specs=(P("rcv", "src", None), P("src"), P("rcv", None)),
        out_specs=P("src", None, "rcv"),
        check_vma=False,
    )
```

```python
import functools
import math

import jax
import jax.numpy as jnp
import ml_dtypes
import numpy as np
from jax import lax
from jax.experimental import pallas as pl
from jax.experimental.pallas import tpu as pltpu
from jax.sharding import PartitionSpec as P

LAGH = 100
BINS = 8
GROUPS_STEP = 16
INVERT = 2
VMEM = 60 * 1024 * 1024


def padded_groups(length):
    groups = -(-(length // 2 + 1) // BINS)
    return -(-groups // (GROUPS_STEP * INVERT)) * GROUPS_STEP * INVERT


def make_tables(length):
    half = length // 2
    pad = padded_groups(length) * BINS
    bins = np.arange(1, half + 1)
    unit = np.float32(2.0 * math.pi / length)
    phase = (bins[:, None] * np.arange(length)[None, :] % length).astype(np.float32) * unit
    forward = np.zeros((2, pad, length), np.float32)
    forward[0, :half] = np.cos(phase)
    forward[1, :half] = -np.sin(phase)
    lags = np.arange(-LAGH, LAGH + 1)
    phase = (lags[:, None] * bins[None, :] % length).astype(np.float32) * unit
    weights = np.where(bins == half, 1.0, 2.0).astype(np.float32) / np.sqrt(np.float32(half))
    nlag = 2 * LAGH + 1
    inverse = np.zeros((-(-nlag // 16) * 16, 2, pad), np.float32)
    inverse[:nlag, 0, :half] = weights * np.cos(phase)
    inverse[:nlag, 1, :half] = -weights * np.sin(phase)
    step = GROUPS_STEP * BINS
    inverse[nlag, 0, half] = 1.0
    inverse = inverse.reshape(-1, 2, pad // step // INVERT, INVERT, step).transpose(2, 0, 3, 1, 4)
    inverse = inverse.reshape(pad // step // INVERT, -1, INVERT * 2 * step)
    return forward.astype(ml_dtypes.bfloat16), inverse.astype(ml_dtypes.bfloat16)


def whiten_kernel(half, seg, forward_ref, traces_ref, quality_ref, out_ref, spec, power):
    step = pl.program_id(0)
    rows = forward_ref.shape[1]
    width = traces_ref.shape[2]
    cols = seg * width
    part = lax.dot_general(
        forward_ref[...].reshape(2 * rows, -1),
        jnp.concatenate([traces_ref[s] for s in range(seg)], axis=1),
        (((1,), (0,)), ((), ())),
        preferred_element_type=jnp.float32,
    )
    re, im = part[:rows], part[rows:]
    start = pl.multiple_of(step * rows, rows)
    spec[0, pl.ds(start, rows), :] = re
    spec[1, pl.ds(start, rows), :] = im
    total = jnp.sum((re * re + im * im).reshape(rows // 8, 8, cols), axis=0)

    @pl.when(step == 0)
    def _():
        power[...] = total

    @pl.when(step > 0)
    def _():
        power[...] += total

    @pl.when(step == pl.num_programs(0) - 1)
    def _():
        mean = jnp.sum(power[...], axis=0, keepdims=True) * (1.0 / half)
        level = 0.5 * jnp.sqrt(mean + 1e-06)
        first_row = lax.axis_index("src") * seg
        qual = jnp.concatenate(
            [quality_ref[pl.ds(first_row + s, 1), :] for s in range(seg)], axis=1
        ).astype(jnp.float32)

        def one_group(g, carry):
            at = pl.ds(pl.multiple_of(g * BINS, BINS), BINS)
            re, im = spec[0, at, :], spec[1, at, :]
            scale = qual / jnp.maximum(jnp.sqrt(re * re + im * im), level)
            parts = []
            for value in (re * scale, im * scale):
                for s in range(seg):
                    parts.append(value[:, s * width : (s + 1) * width])
            out_ref[g] = jnp.concatenate(parts, axis=0).astype(jnp.bfloat16)
            return carry

        lax.fori_loop(0, half // BINS, one_group, 0, unroll=5)
        first = lax.broadcasted_iota(jnp.int32, (BINS, width), 0) == 0
        parts = [jnp.where(first, qual[:, s * width : (s + 1) * width], 0.0) for s in range(seg)]
        parts += [jnp.zeros_like(part) for part in parts]
        out_ref[half // BINS] = jnp.concatenate(parts, axis=0).astype(jnp.bfloat16)
        for g in range(half // BINS + 1, out_ref.shape[0]):
            out_ref[g] = jnp.zeros(out_ref.shape[1:], jnp.bfloat16)


def whiten(traces, quality, forward):
    rows, seg, length = traces.shape
    pad = forward.shape[1]
    steps = 4
    cols = rows * seg
    return pl.pallas_call(
        functools.partial(whiten_kernel, length // 2, seg),
        grid=(steps,),
        in_specs=[
            pl.BlockSpec((2, pad // steps, length), lambda i: (0, i, 0)),
            pl.BlockSpec((seg, length, rows), lambda i: (0, 0, 0)),
            pl.BlockSpec((quality.shape[1], rows), lambda i: (0, 0)),
        ],
        out_specs=pl.BlockSpec((pad // BINS, 2 * seg * BINS, rows), lambda i: (0, 0, 0)),
        out_shape=jax.ShapeDtypeStruct((pad // BINS, 2 * seg * BINS, rows), jnp.bfloat16),
        scratch_shapes=[
            pltpu.VMEM((2, pad, cols), jnp.float32),
            pltpu.VMEM((8, cols), jnp.float32),
        ],
        compiler_params=pltpu.CompilerParams(vmem_limit_bytes=VMEM),
        name="whiten",
    )(forward, traces.transpose(1, 2, 0), quality.T)


def other(a, bit):
    low, high = a % 2, a // 2
    return high * 2 + 1 - low if bit == 0 else (1 - high) * 2 + low


def stack_kernel(
    blocks, each, white_ref, index_ref, inverse_ref, acc,
    ybuf, xbuf, xf, cross, own_sem, core_sems, y_send, y_recv, z_send, z_recv, p_send, p_recv,
):
    parts, _, depth, width = ybuf.shape
    full = parts * depth
    _, _, chunks, rows16, lanes = xbuf.shape
    groups = GROUPS_STEP
    rep = groups * full // lanes
    nsrc = each * blocks
    outer = blocks // 2
    half_k = groups * BINS
    a, b = lax.axis_index("src"), lax.axis_index("rcv")
    core, far = other(a, 0), other(a, 1)
    diag = other(far, 0)
    line, side = b // 2, b % 2
    mate = line * 2 + 1 - side

    barrier = pltpu.get_barrier_semaphore()
    peers = [{"src": core}, {"src": far}, {"rcv": mate}]
    peers += [{"rcv": ((line + d) % outer) * 2 + side} for d in range(1, outer)]
    for peer in peers:
        pl.semaphore_signal(barrier, inc=1, device_id=peer, device_id_type=pl.DeviceIdType.MESH)
    pl.semaphore_wait(barrier, len(peers))

    def groups_of(c):
        return pl.ds(c * groups, groups)

    def own_copy():
        return pltpu.make_async_copy(white_ref, ybuf.at[a], own_sem)

    def send(src, dst, send_sem, recv_sem, device):
        return pltpu.make_async_remote_copy(
            src_ref=src, dst_ref=dst, send_sem=send_sem, recv_sem=recv_sem,
            device_id=device, device_id_type=pl.DeviceIdType.MESH,
        )

    def y_copy(c, kind):
        at = groups_of(c)
        if kind == 1:
            src, dst = ybuf.at[far, at], ybuf.at[far, at]
        else:
            src, dst = white_ref.at[at], ybuf.at[a, at]
        return send(
            src, dst, y_send.at[c, kind], y_recv.at[c, kind], {"src": far if kind == 0 else core}
        )

    def y_wait(c, kind):
        at = groups_of(c)
        got = (far, diag)[kind]
        send(
            ybuf.at[got, at], ybuf.at[got, at], y_send.at[c, kind], y_recv.at[c, kind],
            {"src": far if kind == 0 else core},
        ).wait_recv()

    def core_copy():
        return send(white_ref, ybuf.at[a], core_sems.at[0], core_sems.at[1], {"src": core})

    def core_wait():
        send(
            ybuf.at[core], ybuf.at[core], core_sems.at[0], core_sems.at[1], {"src": core}
        ).wait_recv()

    def z_copy(c, d):
        there = (line + d) % outer
        block = xbuf.at[side, line, c]
        return send(block, block, z_send.at[c, d], z_recv.at[c, d], {"rcv": there * 2 + side})

    def z_wait(c, d):
        start = (line + outer - d) % outer
        block = xbuf.at[side, start, c]
        send(
            block, block, z_send.at[c, d], z_recv.at[c, d], {"rcv": start * 2 + side}
        ).wait_recv()

    def p_copy(c):
        block = xbuf.at[side, :, c]
        return send(block, block, p_send.at[c], p_recv.at[c], {"rcv": mate})

    def p_wait(c):
        block = xbuf.at[1 - side, :, c]
        send(block, block, p_send.at[c], p_recv.at[c], {"rcv": mate}).wait_recv()

    def start_own(c, carry):
        y_copy(c, 0).start()
        return carry

    core_copy().start()
    lax.fori_loop(0, chunks, start_own, 0)
    own_copy().start()
    acc[...] = jnp.zeros_like(acc)
    own_copy().wait()

    row16 = lax.broadcasted_iota(jnp.int32, (rows16, full), 0)
    lane = lax.broadcasted_iota(jnp.int32, (BINS, full), 1)
    row = lax.broadcasted_iota(jnp.int32, (BINS, full), 0)
    mask = lane % BINS == row

    source = jnp.zeros((rows16, width), jnp.int32)
    number = lax.broadcasted_iota(jnp.int32, (rows16, width), 0) % each
    for n in range(each):
        source = jnp.where(number == n, index_ref[n * blocks + b], source)
    channel = b * width + lax.broadcasted_iota(jnp.int32, (rows16, width), 1)
    onehot = jnp.where(source == channel, 1.0, 0.0).astype(jnp.bfloat16)

    def pick(c):
        for t in range(groups // rep):
            found = None
            for sub in range(rep):
                block = ybuf[:, c * groups + t * rep + sub].reshape(full, width)
                part = lax.dot_general(
                    onehot, block, (((1,), (1,)), ((), ())),
                    preferred_element_type=jnp.float32,
                )
                found = part if sub == 0 else jnp.where(row16 // each == sub, part, found)
            xbuf[side, line, c, :, t * full : (t + 1) * full] = found.astype(jnp.bfloat16)

    def multiply(c):
        xf[...] = xbuf[:, :, c].astype(jnp.float32)

        def one_step(t, carry):
            cols = pl.ds(pl.multiple_of(t * full, full), full)
            for sub in range(rep):
                y = ybuf[:, c * groups + t * rep + sub].reshape(parts, 2, depth // 2, width)
                turned = jnp.concatenate([-y[:, 1:], y[:, :1]], axis=1)
                right = jnp.concatenate(
                    [y.reshape(full, width), turned.reshape(full, width)], axis=1
                )
                left = []
                for n in range(each):
                    r = sub * each + n
                    for k in range(blocks):
                        left.append(jnp.where(mask, xf[k % 2, k // 2, r : r + 1, cols], 0.0))
                left = jnp.concatenate(left, axis=0).astype(jnp.bfloat16)
                prod = jnp.dot(left, right, preferred_element_type=jnp.float32)
                prod = prod.reshape(nsrc, BINS, 2 * width)
                at = pl.multiple_of(c % INVERT * 2 * half_k + (t * rep + sub) * BINS, BINS)
                cross[:, pl.ds(at, BINS), :] = prod[:, :, :width]
                cross[:, pl.ds(half_k + at, BINS), :] = prod[:, :, width:]
            return carry

        lax.fori_loop(0, groups // rep, one_step, 0, unroll=2)

    def invert(c):
        table = inverse_ref[c // INVERT]

        def add_pair(p, carry):
            right = jnp.concatenate([cross[2 * p], cross[2 * p + 1]], axis=1).astype(jnp.bfloat16)
            lagged = jnp.dot(table, right, preferred_element_type=jnp.float32)
            acc[2 * p] += lagged[:, :width]
            acc[2 * p + 1] += lagged[:, width:]
            return carry

        lax.fori_loop(0, nsrc // 2, add_pair, 0, unroll=4)

    def one_chunk(c, carry):
        @pl.when(c < chunks)
        def _():
            y_wait(c, 0)
            y_copy(c, 1).start()

        @pl.when(jnp.logical_and(c >= 1, c <= chunks))
        def _():
            pl.when(c == 1)(core_wait)
            y_wait(c - 1, 1)
            pick(c - 1)
            for d in range(1, outer):
                z_copy(c - 1, d).start()

        @pl.when(jnp.logical_and(c >= 2, c <= chunks + 1))
        def _():
            for d in range(1, outer):
                z_wait(c - 2, d)
            p_copy(c - 2).start()

        @pl.when(c >= 3)
        def _():
            p_wait(c - 3)
            multiply(c - 3)

            @pl.when((c - 3) % INVERT == INVERT - 1)
            def _():
                invert(c - 3)

        return carry

    lax.fori_loop(0, chunks + 3, one_chunk, 0)

    def drain(c, carry):
        for kind in range(2):
            y_copy(c, kind).wait_send()
        for d in range(1, outer):
            z_copy(c, d).wait_send()
        p_copy(c).wait_send()
        return carry

    core_copy().wait_send()

    lax.fori_loop(0, chunks, drain, 0)


def stack(white, src_index, inverse, parts, blocks):
    total, depth, rows = white.shape
    steps, taps, depth_k = inverse.shape
    chunks = steps * INVERT
    nsrc = src_index.shape[0]
    each = nsrc // blocks
    rep = 16 // each
    lanes = GROUPS_STEP * parts * depth // rep
    outer = blocks // 2
    flops = 2 * nsrc * rows * total * (BINS * parts * depth * 2 + 2 * BINS * taps)
    return pl.pallas_call(
        functools.partial(stack_kernel, blocks, each),
        in_specs=[
            pl.BlockSpec(memory_space=pl.ANY),
            pl.BlockSpec(memory_space=pltpu.SMEM),
            pl.BlockSpec(memory_space=pltpu.VMEM),
        ],
        out_specs=pl.BlockSpec(memory_space=pltpu.VMEM),
        out_shape=jax.ShapeDtypeStruct((nsrc, taps, rows), jnp.float32),
        scratch_shapes=[
            pltpu.VMEM((parts, total, depth, rows), jnp.bfloat16),
            pltpu.VMEM((2, outer, chunks, 16, lanes), jnp.bfloat16),
            pltpu.VMEM((2, outer, 16, lanes), jnp.float32),
            pltpu.VMEM((nsrc, depth_k, rows), jnp.float32),
            pltpu.SemaphoreType.DMA,
            pltpu.SemaphoreType.DMA((2,)),
            pltpu.SemaphoreType.DMA((chunks, 2)),
            pltpu.SemaphoreType.DMA((chunks, 2)),
            pltpu.SemaphoreType.DMA((chunks, outer)),
            pltpu.SemaphoreType.DMA((chunks, outer)),
            pltpu.SemaphoreType.DMA((chunks,)),
            pltpu.SemaphoreType.DMA((chunks,)),
        ],
        compiler_params=pltpu.CompilerParams(
            vmem_limit_bytes=VMEM, collective_id=0, has_side_effects=True
        ),
        cost_estimate=pl.CostEstimate(flops=flops, bytes_accessed=20_000_000, transcendentals=0),
        name="stack",
    )(white, src_index, inverse)


def finish_kernel(acc_ref, out_ref):
    nlag = out_ref.shape[0]
    value = acc_ref[...]
    scale = 1.0 / jnp.maximum(value[:, nlag : nlag + 1, :], 1.0)
    out_ref[...] = jnp.swapaxes(value * scale, 0, 1)[:nlag]


def finish(acc):
    nsrc, taps, rows = acc.shape
    nlag, tile = 2 * LAGH + 1, 16
    return pl.pallas_call(
        finish_kernel,
        grid=(nsrc // tile,),
        in_specs=[pl.BlockSpec((tile, taps, rows), lambda i: (i, 0, 0))],
        out_specs=pl.BlockSpec((nlag, tile, rows), lambda i: (0, i, 0)),
        out_shape=jax.ShapeDtypeStruct((nlag, nsrc, rows), jnp.float32),
        compiler_params=pltpu.CompilerParams(vmem_limit_bytes=VMEM),
        name="finish",
    )(acc)


def on_device(parts, blocks, traces, src_index, quality):
    forward, inverse = make_tables(traces.shape[2])
    white = whiten(traces, quality, jnp.asarray(forward))
    return finish(stack(white, src_index, jnp.asarray(inverse), parts, blocks)).transpose(1, 0, 2)


def solution(mesh):
    return jax.shard_map(
        functools.partial(on_device, mesh.shape["src"], mesh.shape["rcv"]),
        mesh=mesh,
        in_specs=(P("rcv", "src", None), P("src"), P("rcv", None)),
        out_specs=P("src", None, "rcv"),
        check_vma=False,
    )
```

```python
import functools
import math

import jax
import jax.numpy as jnp
import ml_dtypes
import numpy as np
from jax import lax
from jax.experimental import pallas as pl
from jax.experimental.pallas import tpu as pltpu
from jax.sharding import PartitionSpec as P

LAGH = 100
BINS = 8
GROUPS_STEP = 16
INVERT = 2
VMEM = 60 * 1024 * 1024


def padded_groups(length):
    groups = -(-(length // 2 + 1) // BINS)
    return -(-groups // (GROUPS_STEP * INVERT)) * GROUPS_STEP * INVERT


def make_tables(length):
    half = length // 2
    pad = padded_groups(length) * BINS
    bins = np.arange(1, half + 1)
    unit = np.float32(2.0 * math.pi / length)
    phase = (bins[:, None] * np.arange(length)[None, :] % length).astype(np.float32) * unit
    forward = np.zeros((2, pad, length), np.float32)
    forward[0, :half] = np.cos(phase)
    forward[1, :half] = -np.sin(phase)
    lags = np.arange(-LAGH, LAGH + 1)
    phase = (lags[:, None] * bins[None, :] % length).astype(np.float32) * unit
    weights = np.where(bins == half, 1.0, 2.0).astype(np.float32) / np.sqrt(np.float32(half))
    nlag = 2 * LAGH + 1
    inverse = np.zeros((-(-nlag // 16) * 16, 2, pad), np.float32)
    inverse[:nlag, 0, :half] = weights * np.cos(phase)
    inverse[:nlag, 1, :half] = -weights * np.sin(phase)
    step = GROUPS_STEP * BINS
    inverse[nlag, 0, half] = 1.0
    inverse = inverse.reshape(-1, 2, pad // step // INVERT, INVERT, step).transpose(2, 0, 3, 1, 4)
    inverse = inverse.reshape(pad // step // INVERT, -1, INVERT * 2 * step)
    return forward.astype(ml_dtypes.bfloat16), inverse.astype(ml_dtypes.bfloat16)


def whiten_kernel(half, seg, forward_ref, traces_ref, quality_ref, out_ref, spec, power):
    step = pl.program_id(0)
    rows = forward_ref.shape[1]
    width = traces_ref.shape[2]
    cols = seg * width
    part = lax.dot_general(
        forward_ref[...].reshape(2 * rows, -1),
        jnp.concatenate([traces_ref[s] for s in range(seg)], axis=1),
        (((1,), (0,)), ((), ())),
        preferred_element_type=jnp.float32,
    )
    re, im = part[:rows], part[rows:]
    start = pl.multiple_of(step * rows, rows)
    spec[0, pl.ds(start, rows), :] = re
    spec[1, pl.ds(start, rows), :] = im
    total = jnp.sum((re * re + im * im).reshape(rows // 8, 8, cols), axis=0)

    @pl.when(step == 0)
    def _():
        power[...] = total

    @pl.when(step > 0)
    def _():
        power[...] += total

    @pl.when(step == pl.num_programs(0) - 1)
    def _():
        mean = jnp.sum(power[...], axis=0, keepdims=True) * (1.0 / half)
        level = 0.5 * jnp.sqrt(mean + 1e-06)
        first_row = lax.axis_index("src") * seg
        qual = jnp.concatenate(
            [quality_ref[pl.ds(first_row + s, 1), :] for s in range(seg)], axis=1
        ).astype(jnp.float32)

        def one_group(g, carry):
            at = pl.ds(pl.multiple_of(g * BINS, BINS), BINS)
            re, im = spec[0, at, :], spec[1, at, :]
            scale = qual / jnp.maximum(jnp.sqrt(re * re + im * im), level)
            parts = []
            for value in (re * scale, im * scale):
                for s in range(seg):
                    parts.append(value[:, s * width : (s + 1) * width])
            out_ref[g] = jnp.concatenate(parts, axis=0).astype(jnp.bfloat16)
            return carry

        lax.fori_loop(0, half // BINS, one_group, 0, unroll=5)
        first = lax.broadcasted_iota(jnp.int32, (BINS, width), 0) == 0
        parts = [jnp.where(first, qual[:, s * width : (s + 1) * width], 0.0) for s in range(seg)]
        parts += [jnp.zeros_like(part) for part in parts]
        out_ref[half // BINS] = jnp.concatenate(parts, axis=0).astype(jnp.bfloat16)
        for g in range(half // BINS + 1, out_ref.shape[0]):
            out_ref[g] = jnp.zeros(out_ref.shape[1:], jnp.bfloat16)


def whiten(traces, quality, forward):
    rows, seg, length = traces.shape
    pad = forward.shape[1]
    steps = 4
    cols = rows * seg
    return pl.pallas_call(
        functools.partial(whiten_kernel, length // 2, seg),
        grid=(steps,),
        in_specs=[
            pl.BlockSpec((2, pad // steps, length), lambda i: (0, i, 0)),
            pl.BlockSpec((seg, length, rows), lambda i: (0, 0, 0)),
            pl.BlockSpec((quality.shape[1], rows), lambda i: (0, 0)),
        ],
        out_specs=pl.BlockSpec((pad // BINS, 2 * seg * BINS, rows), lambda i: (0, 0, 0)),
        out_shape=jax.ShapeDtypeStruct((pad // BINS, 2 * seg * BINS, rows), jnp.bfloat16),
        scratch_shapes=[
            pltpu.VMEM((2, pad, cols), jnp.float32),
            pltpu.VMEM((8, cols), jnp.float32),
        ],
        compiler_params=pltpu.CompilerParams(vmem_limit_bytes=VMEM),
        name="whiten",
    )(forward, traces.transpose(1, 2, 0), quality.T)


def other(a, bit):
    low, high = a % 2, a // 2
    return high * 2 + 1 - low if bit == 0 else (1 - high) * 2 + low


def stack_kernel(
    blocks, each, white_ref, index_ref, inverse_ref, acc,
    ybuf, xbuf, xf, cross, own_sem, y_send, y_recv, z_send, z_recv, p_send, p_recv,
):
    parts, _, depth, width = ybuf.shape
    full = parts * depth
    _, chunks, rows16, lanes = xbuf.shape
    groups = GROUPS_STEP
    rep = groups * full // lanes
    nsrc = each * blocks
    outer = blocks // 2
    half_k = groups * BINS
    a, b = lax.axis_index("src"), lax.axis_index("rcv")
    core, far = other(a, 0), other(a, 1)
    diag = other(far, 0)
    line, side = b // 2, b % 2
    mate = line * 2 + 1 - side

    barrier = pltpu.get_barrier_semaphore()
    peers = [{"src": core}, {"src": far}, {"rcv": mate}]
    peers += [{"rcv": ((line + d) % outer) * 2 + side} for d in range(1, outer)]
    for peer in peers:
        pl.semaphore_signal(barrier, inc=1, device_id=peer, device_id_type=pl.DeviceIdType.MESH)
    pl.semaphore_wait(barrier, len(peers))

    def groups_of(c):
        return pl.ds(c * groups, groups)

    def own_copy():
        return pltpu.make_async_copy(white_ref, ybuf.at[a], own_sem)

    def send(src, dst, send_sem, recv_sem, device):
        return pltpu.make_async_remote_copy(
            src_ref=src, dst_ref=dst, send_sem=send_sem, recv_sem=recv_sem,
            device_id=device, device_id_type=pl.DeviceIdType.MESH,
        )

    def y_copy(c, kind):
        at = groups_of(c)
        if kind == 2:
            src, dst = ybuf.at[far, at], ybuf.at[far, at]
        else:
            src, dst = white_ref.at[at], ybuf.at[a, at]
        return send(
            src, dst, y_send.at[c, kind], y_recv.at[c, kind], {"src": far if kind == 0 else core}
        )

    def y_wait(c, kind):
        at = groups_of(c)
        got = (far, core, diag)[kind]
        send(
            ybuf.at[got, at], ybuf.at[got, at], y_send.at[c, kind], y_recv.at[c, kind],
            {"src": far if kind == 0 else core},
        ).wait_recv()

    def z_copy(c, d):
        there = ((line + d) % outer) * 2 + side
        return send(xbuf.at[b, c], xbuf.at[b, c], z_send.at[c, d], z_recv.at[c, d], {"rcv": there})

    def z_wait(c, d):
        start = ((line + outer - d) % outer) * 2 + side
        send(
            xbuf.at[start, c], xbuf.at[start, c], z_send.at[c, d], z_recv.at[c, d], {"rcv": start}
        ).wait_recv()

    def p_copy(c, d):
        start = ((line + outer - d) % outer) * 2 + side
        return send(
            xbuf.at[start, c], xbuf.at[start, c], p_send.at[c, d], p_recv.at[c, d], {"rcv": mate}
        )

    def p_wait(c, d):
        start = ((line + outer - d) % outer) * 2 + 1 - side
        send(
            xbuf.at[start, c], xbuf.at[start, c], p_send.at[c, d], p_recv.at[c, d], {"rcv": mate}
        ).wait_recv()

    def start_own(c, carry):
        y_copy(c, 0).start()
        y_copy(c, 1).start()
        return carry

    lax.fori_loop(0, chunks, start_own, 0)
    own_copy().start()
    acc[...] = jnp.zeros_like(acc)
    own_copy().wait()

    row16 = lax.broadcasted_iota(jnp.int32, (rows16, full), 0)
    lane = lax.broadcasted_iota(jnp.int32, (BINS, full), 1)
    row = lax.broadcasted_iota(jnp.int32, (BINS, full), 0)
    mask = lane % BINS == row

    source = jnp.zeros((rows16, width), jnp.int32)
    number = lax.broadcasted_iota(jnp.int32, (rows16, width), 0) % each
    for n in range(each):
        source = jnp.where(number == n, index_ref[n * blocks + b], source)
    channel = b * width + lax.broadcasted_iota(jnp.int32, (rows16, width), 1)
    onehot = jnp.where(source == channel, 1.0, 0.0).astype(jnp.bfloat16)

    def pick(c):
        for t in range(groups // rep):
            found = None
            for sub in range(rep):
                block = ybuf[:, c * groups + t * rep + sub].reshape(full, width)
                part = lax.dot_general(
                    onehot, block, (((1,), (1,)), ((), ())),
                    preferred_element_type=jnp.float32,
                )
                found = part if sub == 0 else jnp.where(row16 // each == sub, part, found)
            xbuf[b, c, :, t * full : (t + 1) * full] = found.astype(jnp.bfloat16)

    def multiply(c):
        xf[...] = xbuf[:, c].astype(jnp.float32)

        def one_step(t, carry):
            cols = pl.ds(pl.multiple_of(t * full, full), full)
            for sub in range(rep):
                y = ybuf[:, c * groups + t * rep + sub].reshape(parts, 2, depth // 2, width)
                turned = jnp.concatenate([-y[:, 1:], y[:, :1]], axis=1)
                right = jnp.concatenate(
                    [y.reshape(full, width), turned.reshape(full, width)], axis=1
                )
                left = []
                for n in range(each):
                    r = sub * each + n
                    for k in range(blocks):
                        left.append(jnp.where(mask, xf[k, r : r + 1, cols], 0.0))
                left = jnp.concatenate(left, axis=0).astype(jnp.bfloat16)
                prod = jnp.dot(left, right, preferred_element_type=jnp.float32)
                prod = prod.reshape(nsrc, BINS, 2 * width)
                at = pl.multiple_of(c % INVERT * 2 * half_k + (t * rep + sub) * BINS, BINS)
                cross[:, pl.ds(at, BINS), :] = prod[:, :, :width]
                cross[:, pl.ds(half_k + at, BINS), :] = prod[:, :, width:]
            return carry

        lax.fori_loop(0, groups // rep, one_step, 0, unroll=4)

    def invert(c):
        table = inverse_ref[c // INVERT]

        def add_pair(p, carry):
            right = jnp.concatenate([cross[2 * p], cross[2 * p + 1]], axis=1).astype(jnp.bfloat16)
            lagged = jnp.dot(table, right, preferred_element_type=jnp.float32)
            acc[2 * p] += lagged[:, :width]
            acc[2 * p + 1] += lagged[:, width:]
            return carry

        lax.fori_loop(0, nsrc // 2, add_pair, 0, unroll=8)

    def one_chunk(c, carry):
        @pl.when(c < chunks)
        def _():
            y_wait(c, 0)
            y_copy(c, 2).start()

        @pl.when(jnp.logical_and(c >= 1, c <= chunks))
        def _():
            y_wait(c - 1, 1)
            y_wait(c - 1, 2)
            pick(c - 1)
            for d in range(1, outer):
                z_copy(c - 1, d).start()
            p_copy(c - 1, 0).start()

        @pl.when(jnp.logical_and(c >= 2, c <= chunks + 1))
        def _():
            for d in range(1, outer):
                z_wait(c - 2, d)
                p_copy(c - 2, d).start()

        @pl.when(c >= 3)
        def _():
            for d in range(outer):
                p_wait(c - 3, d)
            multiply(c - 3)

            @pl.when((c - 3) % INVERT == INVERT - 1)
            def _():
                invert(c - 3)

        return carry

    lax.fori_loop(0, chunks + 3, one_chunk, 0)

    def drain(c, carry):
        for kind in range(3):
            y_copy(c, kind).wait_send()
        for d in range(1, outer):
            z_copy(c, d).wait_send()
        for d in range(outer):
            p_copy(c, d).wait_send()
        return carry

    lax.fori_loop(0, chunks, drain, 0)


def stack(white, src_index, inverse, parts, blocks):
    total, depth, rows = white.shape
    steps, taps, depth_k = inverse.shape
    chunks = steps * INVERT
    nsrc = src_index.shape[0]
    each = nsrc // blocks
    rep = 16 // each
    lanes = GROUPS_STEP * parts * depth // rep
    outer = blocks // 2
    flops = 2 * nsrc * rows * total * (BINS * parts * depth * 2 + 2 * BINS * taps)
    return pl.pallas_call(
        functools.partial(stack_kernel, blocks, each),
        in_specs=[
            pl.BlockSpec(memory_space=pl.ANY),
            pl.BlockSpec(memory_space=pltpu.SMEM),
            pl.BlockSpec(memory_space=pltpu.VMEM),
        ],
        out_specs=pl.BlockSpec(memory_space=pltpu.VMEM),
        out_shape=jax.ShapeDtypeStruct((nsrc, taps, rows), jnp.float32),
        scratch_shapes=[
            pltpu.VMEM((parts, total, depth, rows), jnp.bfloat16),
            pltpu.VMEM((blocks, chunks, 16, lanes), jnp.bfloat16),
            pltpu.VMEM((blocks, 16, lanes), jnp.float32),
            pltpu.VMEM((nsrc, depth_k, rows), jnp.float32),
            pltpu.SemaphoreType.DMA,
            pltpu.SemaphoreType.DMA((chunks, 3)),
            pltpu.SemaphoreType.DMA((chunks, 3)),
            pltpu.SemaphoreType.DMA((chunks, outer)),
            pltpu.SemaphoreType.DMA((chunks, outer)),
            pltpu.SemaphoreType.DMA((chunks, outer)),
            pltpu.SemaphoreType.DMA((chunks, outer)),
        ],
        compiler_params=pltpu.CompilerParams(
            vmem_limit_bytes=VMEM, collective_id=0, has_side_effects=True
        ),
        cost_estimate=pl.CostEstimate(flops=flops, bytes_accessed=20_000_000, transcendentals=0),
        name="stack",
    )(white, src_index, inverse)


def finish_kernel(acc_ref, out_ref):
    nlag = out_ref.shape[0]
    value = acc_ref[...]
    scale = 1.0 / jnp.maximum(value[:, nlag : nlag + 1, :], 1.0)
    out_ref[...] = jnp.swapaxes(value * scale, 0, 1)[:nlag]


def finish(acc):
    nsrc, taps, rows = acc.shape
    nlag, tile = 2 * LAGH + 1, 16
    return pl.pallas_call(
        finish_kernel,
        grid=(nsrc // tile,),
        in_specs=[pl.BlockSpec((tile, taps, rows), lambda i: (i, 0, 0))],
        out_specs=pl.BlockSpec((nlag, tile, rows), lambda i: (0, i, 0)),
        out_shape=jax.ShapeDtypeStruct((nlag, nsrc, rows), jnp.float32),
        compiler_params=pltpu.CompilerParams(vmem_limit_bytes=VMEM),
        name="finish",
    )(acc)


def on_device(parts, blocks, traces, src_index, quality):
    forward, inverse = make_tables(traces.shape[2])
    white = whiten(traces, quality, jnp.asarray(forward))
    return finish(stack(white, src_index, jnp.asarray(inverse), parts, blocks)).transpose(1, 0, 2)


def solution(mesh):
    return jax.shard_map(
        functools.partial(on_device, mesh.shape["src"], mesh.shape["rcv"]),
        mesh=mesh,
        in_specs=(P("rcv", "src", None), P("src"), P("rcv", None)),
        out_specs=P("src", None, "rcv"),
        check_vma=False,
    )
```
